32 devices in a mesh: ctxa: 8 (over z, x), ctxb: 4 (over y, core).
Axes of the slice: x: 2, y: 2, z: 4, core: 2. Of those that a mesh axis runs over, the one named last changes fastest.
Arguments:
- tokens: bfloat16 [4096, 1024], P(('ctxa', 'ctxb')), may hold values from -80 to 80
- w_query: bfloat16 [1024, 512], replicated, may hold values from -0.1875 to 0.1875
- w_key: bfloat16 [1024, 512], replicated, may hold values from -0.1875 to 0.1875
- w_value: bfloat16 [1024, 512], replicated, may hold values from -0.1875 to 0.1875
- w_slot: bfloat16 [8, 64, 128], replicated, may hold values from -3 to 3
- w_out: bfloat16 [512, 1024], replicated, may hold values from -1 to 1
Outputs:
- mixed: bfloat16 [4096, 1024], P(('ctxa', 'ctxb'))
The draws below stay inside these ranges and needn't reach their ends.
All inputs are finite; a program needn't handle non-finite values.
Results may differ from the reference program's by a relative error of at most 0.012.
The reference program's roundings to bfloat16 on the way count: a program that leaves them out, or rounds other values in their place, can miss the bound.
Values may be sent and summed in bfloat16 or wider, within the bound.
No kernel may reach another device: no remote copies, remote signals or barrier semaphores. Data moves between devices by JAX's collectives and lax.ppermute only.
A program may use at most 192 MiB of HBM per device.

```python
import jax
import jax.numpy as jnp
from jax import lax

D = 1024
HEADS = 8
HEAD_DIM = 64
SLOTS = 128
WINDOW = 128
TOK_DEV = 128
SEQ = 4096


def draw_tokens(key, part):
    keys = jax.random.split(jax.random.fold_in(key, 11), 1)
    base = jnp.clip(jax.random.normal(keys[0], (SEQ, D), jnp.float32), -6.0, 6.0)
    return base.astype(jnp.bfloat16)


def centred(rng, extent, scale, reach, held_as=jnp.bfloat16):
    drawn = scale * jax.random.normal(rng, extent, jnp.float32)
    return jnp.clip(drawn, min=-reach, max=reach).astype(held_as)


def setup_inputs(seed: int = 0) -> dict:
    splits = jax.random.split(jax.random.key(seed), 7)
    tokens = draw_tokens(jax.random.fold_in(splits[6], 71), 0)
    w_query = centred(splits[1], (D, HEADS * HEAD_DIM), D ** -0.5, 0.1875)
    w_key = centred(splits[2], (D, HEADS * HEAD_DIM), D ** -0.5, 0.1875)
    w_value = centred(splits[3], (D, HEADS * HEAD_DIM), D ** -0.5, 0.1875)
    w_slot = centred(splits[4], (HEADS, HEAD_DIM, SLOTS), 0.5, 3.0)
    w_out = centred(splits[5], (HEADS * HEAD_DIM, D), (HEADS * HEAD_DIM // 16) ** -0.5, 1.0)
    return {"tokens": tokens, "w_query": w_query, "w_key": w_key, "w_value": w_value, "w_slot": w_slot, "w_out": w_out}


def layer_norm(values):
    center = values - lax.optimization_barrier(jnp.mean(values, axis=-1, keepdims=True))
    spread = lax.optimization_barrier(jnp.mean(center * center, axis=-1, keepdims=True))
    return center * lax.rsqrt(spread + 1e-05)

def reference(tokens, w_query, w_key, w_value, w_slot, w_out):
    width = HEADS * HEAD_DIM
    query = jnp.dot(tokens, w_query, preferred_element_type=jnp.float32).astype(jnp.bfloat16)
    key = jnp.dot(tokens, w_key, preferred_element_type=jnp.float32).astype(jnp.bfloat16)
    value = jnp.dot(tokens, w_value, preferred_element_type=jnp.float32).astype(jnp.bfloat16)

    def slot_head(head):
        first = (head * HEAD_DIM).astype(jnp.int32)
        key_head = lax.dynamic_slice_in_dim(key, first, HEAD_DIM, 1).astype(jnp.float32)
        value_head = lax.dynamic_slice_in_dim(value, first, HEAD_DIM, 1).astype(jnp.float32)
        slot_map = lax.dynamic_index_in_dim(w_slot, head, 0, keepdims=False).astype(jnp.float32)
        logits = jnp.dot(key_head, slot_map, precision=lax.Precision.HIGHEST)
        top = lax.optimization_barrier(jnp.max(logits, axis=0))
        weight = jnp.exp(logits - top[None, :])
        total = lax.optimization_barrier(jnp.sum(weight, axis=0))
        paired = jnp.concatenate([key_head, value_head], axis=1)
        sums = jnp.dot(weight.T, paired, precision=lax.Precision.HIGHEST)
        slot_keys = layer_norm(sums[:, :HEAD_DIM])
        slot_values = sums[:, HEAD_DIM:] / total[:, None]
        return (slot_keys.astype(jnp.bfloat16), slot_values.astype(jnp.bfloat16))
    slot_keys, slot_values = lax.map(slot_head, jnp.arange(HEADS, dtype=jnp.int32))
    near_keys = layer_norm(key.reshape(SEQ, HEADS, HEAD_DIM).astype(jnp.float32)).astype(jnp.bfloat16)
    near_keys = near_keys.reshape(SEQ, width)
    padded_keys = jnp.pad(near_keys, ((WINDOW, WINDOW), (0, 0)))
    padded_values = jnp.pad(value, ((WINDOW, WINDOW), (0, 0)))
    block = min(512, TOK_DEV)
    span = block + 2 * WINDOW
    scale = 1.0 / HEAD_DIM ** 0.5

    def attend(index):
        start = (index * block).astype(jnp.int32)
        query_block = lax.dynamic_slice_in_dim(query, start, block, 0).reshape(block, HEADS, HEAD_DIM).astype(jnp.float32)
        keys_block = lax.dynamic_slice_in_dim(padded_keys, start, span, 0).reshape(span, HEADS, HEAD_DIM).astype(jnp.float32)
        values_block = lax.dynamic_slice_in_dim(padded_values, start, span, 0).reshape(span, HEADS, HEAD_DIM).astype(jnp.float32)
        query_pos = start + jnp.arange(block, dtype=jnp.int32)
        key_pos = start - WINDOW + jnp.arange(span, dtype=jnp.int32)
        valid = (jnp.abs(key_pos[None, :] - query_pos[:, None]) <= WINDOW) & (key_pos[None, :] >= 0) & (key_pos[None, :] < SEQ)
        near = jnp.einsum('bhd,khd->hbk', query_block, keys_block) * scale
        near = jnp.where(valid[None], near, -1e+30)
        far = jnp.einsum('bhd,hsd->hbs', query_block, slot_keys.astype(jnp.float32)) * scale
        top = jnp.maximum(lax.optimization_barrier(jnp.max(near, axis=-1)), lax.optimization_barrier(jnp.max(far, axis=-1)))
        near_exp = jnp.exp(near - top[..., None])
        far_exp = jnp.exp(far - top[..., None])
        denom = lax.optimization_barrier(jnp.sum(near_exp, axis=-1)) + lax.optimization_barrier(jnp.sum(far_exp, axis=-1))
        near_probs = (near_exp / denom[..., None]).astype(jnp.bfloat16).astype(jnp.float32)
        far_probs = (far_exp / denom[..., None]).astype(jnp.bfloat16).astype(jnp.float32)
        result = jnp.einsum('hbk,khd->bhd', near_probs, values_block)
        result = result + jnp.einsum('hbs,hsd->bhd', far_probs, slot_values.astype(jnp.float32))
        return result.reshape(block, width).astype(jnp.bfloat16)
    attended = lax.map(attend, jnp.arange(SEQ // block, dtype=jnp.int32)).reshape(SEQ, width)
    return jnp.dot(attended, w_out, preferred_element_type=jnp.float32).astype(jnp.bfloat16)
```

```python
import functools

import jax
import jax.numpy as jnp
from jax import lax
from jax.experimental import pallas as pl
from jax.experimental.pallas import tpu as pltpu
from jax.sharding import PartitionSpec as P

AXES = ("ctxa", "ctxb")
SIDE = 16
WINDOW = 128
EPS = 1e-05
BF16 = jnp.bfloat16
F32 = jnp.float32
VMEM = pltpu.VMEM


def dot(a, b, ca=1, cb=0):
    return lax.dot_general(a, b, (((ca,), (cb,)), ((), ())), preferred_element_type=F32)


def pieces(x):
    high = x.astype(BF16)
    rest = x - high.astype(F32)
    mid = rest.astype(BF16)
    return high, mid, (rest - mid.astype(F32)).astype(BF16)


def write_message(msg_ref, h, sums, top, total):
    feats, slots = sums.shape
    msg_ref[h, :feats, :] = sums.astype(BF16)
    rows = [p.astype(F32) for p in pieces(top) + pieces(total)]
    rows.append(jnp.zeros((SIDE - len(rows), slots), F32))
    msg_ref[h, feats:, :] = jnp.concatenate(rows, axis=0).astype(BF16)


def read_message(msg_ref, h, feats):
    sums = msg_ref[h, :feats, :].astype(F32)
    side = msg_ref[h, feats:, :].astype(F32)
    top = side[0:1] + side[1:2] + side[2:3]
    total = side[3:4] + side[4:5] + side[5:6]
    return sums, top, total


def merged(sums_ref, side_ref, msg_ref, h, heads):
    feats = sums_ref.shape[1]
    other, other_top, other_total = read_message(msg_ref, h, feats)
    own_top, own_total = side_ref[h : h + 1, :], side_ref[heads + h : heads + h + 1, :]
    top = jnp.maximum(own_top, other_top)
    a, b = jnp.exp(own_top - top), jnp.exp(other_top - top)
    return sums_ref[h] * a + other * b, top, own_total * a + other_total * b


def slots_kernel(own_ref, par_ref, wk_ref, wv_ref, ws_ref, sums_ref, side_ref, msg_ref, kv_ref):
    heads, dim, _ = ws_ref.shape
    rows = own_ref.shape[0]
    tokens = jnp.concatenate([own_ref[...], par_ref[...]], axis=0)
    key = dot(tokens, wk_ref[...]).astype(BF16)
    value = dot(tokens, wv_ref[...]).astype(BF16)
    key_t, value_t = key.T, value.T
    for h in range(heads):
        cols = slice(h * dim, (h + 1) * dim)
        pair = jnp.concatenate([key_t[cols], value_t[cols]], axis=0)
        kv_ref[h] = pair
        logits = dot(key[:, cols], ws_ref[h])
        top = jnp.max(logits, axis=0, keepdims=True)
        weight = jnp.exp(logits - top)
        total = jnp.sum(weight, axis=0, keepdims=True)
        high = weight.astype(BF16)
        low = (weight - high.astype(F32)).astype(BF16)
        sums = dot(pair, high) + dot(pair, low)
        sums_ref[h] = sums
        side_ref[h : h + 1, :] = top
        side_ref[heads + h : heads + h + 1, :] = total
        write_message(msg_ref, h, sums, top, total)


def combine_kernel(sums_ref, side_ref, msg_ref, sums_out, side_out, msg_out):
    heads = sums_ref.shape[0]
    for h in range(heads):
        sums, top, total = merged(sums_ref, side_ref, msg_ref, h, heads)
        sums_out[h] = sums
        side_out[h : h + 1, :] = top
        side_out[heads + h : heads + h + 1, :] = total
        write_message(msg_out, h, sums, top, total)


def layer_norm_rows(u):
    center = u - jnp.mean(u, axis=0, keepdims=True)
    spread = jnp.mean(center * center, axis=0, keepdims=True)
    return center * lax.rsqrt(spread + EPS)


def query_kernel(own_ref, par_ref, wq_ref, kv_ref, q_ref, own_out, par_out):
    heads, both, _ = kv_ref.shape
    dim = both // 2
    rows = own_ref.shape[0]
    tokens = jnp.concatenate([own_ref[...], par_ref[...]], axis=0)
    q_ref[...] = dot(tokens, wq_ref[...]).astype(BF16).T
    for h in range(heads):
        near = layer_norm_rows(kv_ref[h, :dim, :].astype(F32)).astype(BF16)
        own_out[h, :dim, :] = near[:, :rows]
        par_out[h, :dim, :] = near[:, rows:]
        own_out[h, dim:, :] = kv_ref[h, dim:, :rows]
        par_out[h, dim:, :] = kv_ref[h, dim:, rows:]


def near_kernel(n_dev, q_ref, own_ref, par_ref, hown_ref, hpar_ref, stat_ref, out_ref):
    heads, both, rows = own_ref.shape
    dim = both // 2
    scale = 1.0 / dim**0.5
    me = lax.axis_index(AXES)
    core = me % 2
    u = lax.broadcasted_iota(jnp.int32, (rows, rows), 0)
    t = lax.broadcasted_iota(jnp.int32, (rows, rows), 1)
    flip = 1 - 2 * core
    before = (u - t) * flip >= 0
    after = (u - t) * flip <= 0
    has_own = jnp.where(core == 0, me >= 2, me < n_dev - 2)
    has_par = jnp.where(core == 0, me < n_dev - 2, me >= 2)
    ninf = -1e30
    for h in range(heads):
        for part in range(2):
            mine, other, halo = (own_ref, par_ref, hown_ref) if part == 0 else (par_ref, own_ref, hpar_ref)
            q = q_ref[h * dim : (h + 1) * dim, part * rows : (part + 1) * rows]
            s0 = dot(mine[h, :dim, :], q, 0, 0) * scale
            s1 = dot(other[h, :dim, :], q, 0, 0) * scale
            s2 = dot(halo[h, :dim, :], q, 0, 0) * scale
            if part == 0:
                s1 = jnp.where(after, s1, ninf)
                s2 = jnp.where(before & has_own, s2, ninf)
            else:
                s1 = jnp.where(before, s1, ninf)
                s2 = jnp.where(after & has_par, s2, ninf)
            top = jnp.max(jnp.maximum(jnp.maximum(s0, s1), s2), axis=0, keepdims=True)
            e0, e1, e2 = jnp.exp(s0 - top), jnp.exp(s1 - top), jnp.exp(s2 - top)
            total = jnp.sum(e0 + e1 + e2, axis=0, keepdims=True)
            out = (
                dot(mine[h, dim:, :], e0.astype(BF16))
                + dot(other[h, dim:, :], e1.astype(BF16))
                + dot(halo[h, dim:, :], e2.astype(BF16))
            )
            at = part * heads + h
            stat_ref[at : at + 1, :] = top
            stat_ref[2 * heads + at : 2 * heads + at + 1, :] = total
            out_ref[h, :, part * rows : (part + 1) * rows] = out


def far_kernel(sums_ref, side_ref, msg_ref, q_ref, stat_ref, near_ref, keep_ref, send_ref):
    heads, both, _ = sums_ref.shape
    dim = both // 2
    rows = keep_ref.shape[1]
    scale = 1.0 / dim**0.5
    for h in range(heads):
        sums, _, total = merged(sums_ref, side_ref, msg_ref, h, heads)
        slot_keys = layer_norm_rows(sums[:dim]).astype(BF16)
        slot_values = (sums[dim:] / total).astype(BF16)
        q = q_ref[h * dim : (h + 1) * dim, :]
        far = dot(slot_keys, q, 0, 0) * scale
        near_top = jnp.concatenate([stat_ref[h : h + 1, :], stat_ref[heads + h : heads + h + 1, :]], axis=1)
        near_total = jnp.concatenate(
            [stat_ref[2 * heads + h : 2 * heads + h + 1, :], stat_ref[3 * heads + h : 3 * heads + h + 1, :]], axis=1
        )
        top = jnp.maximum(jnp.max(far, axis=0, keepdims=True), near_top)
        near_scale = jnp.exp(near_top - top)
        e = jnp.exp(far - top)
        denom = jnp.sum(e, axis=0, keepdims=True) + near_total * near_scale
        out = near_ref[h] * near_scale + dot(slot_values, e.astype(BF16))
        out = (out / denom).astype(BF16)
        keep_ref[h * dim : (h + 1) * dim, :] = out[:, :rows]
        send_ref[h * dim : (h + 1) * dim, :] = out[:, rows:]


def mix_kernel(own_ref, other_ref, w_ref, out_ref):
    width = own_ref.shape[0]
    core = lax.axis_index(AXES) % 2
    mine = pl.ds(pl.multiple_of(core * width, width), width)
    theirs = pl.ds(pl.multiple_of((1 - core) * width, width), width)
    out = dot(own_ref[...], w_ref[mine, :], 0, 0) + dot(other_ref[...], w_ref[theirs, :], 0, 0)
    out_ref[...] = out.astype(BF16)


def call(kernel, outs, ins, flops, name):
    spec = pl.BlockSpec(memory_space=VMEM)
    out_shape = [jax.ShapeDtypeStruct(s, d) for s, d in outs]
    size = sum(x.size * x.dtype.itemsize for x in ins) + sum(
        s.size * s.dtype.itemsize for s in out_shape
    )
    result = pl.pallas_call(
        kernel,
        out_shape=out_shape,
        in_specs=[spec] * len(ins),
        out_specs=[spec] * len(outs),
        compiler_params=pltpu.CompilerParams(vmem_limit_bytes=24 * 2**20),
        cost_estimate=pl.CostEstimate(flops=flops, bytes_accessed=size, transcendentals=0),
        name=name,
    )(*ins)
    return result


def per_device(tokens, w_query, w_key, w_value, w_slot, w_out):
    rows = tokens.shape[0]
    count = lax.axis_size(AXES)
    heads, dim, slots = w_slot.shape
    half = heads // 2
    width = half * dim
    core = lax.axis_index(AXES) % 2

    def permute(x, target):
        pairs = [(n, target(n)) for n in range(count) if 0 <= target(n) < count]
        return lax.ppermute(x, AXES, pairs)

    other = permute(tokens, lambda n: n ^ 1)
    cut = lambda w: lax.dynamic_slice_in_dim(w, core * width, width, 1)
    wq, wk, wv = cut(w_query), cut(w_key), cut(w_value)
    ws = lax.dynamic_slice_in_dim(w_slot, core * half, half, 0)
    sums_s, side_s = ((half, 2 * dim, slots), F32), ((2 * half, slots), F32)
    msg_s = ((half, 2 * dim + SIDE, slots), BF16)
    chunk_s = ((half, 2 * dim, rows), BF16)
    sums, side, msg, kv = call(
        slots_kernel,
        [sums_s, side_s, msg_s, ((half, 2 * dim, 2 * rows), BF16)],
        [tokens, other, wk, wv, ws],
        2 * 2 * rows * tokens.shape[1] * width * 2,
        "slots_local",
    )
    q, own, par = call(
        query_kernel,
        [((width, 2 * rows), BF16), chunk_s, chunk_s],
        [tokens, other, wq, kv],
        2 * 2 * rows * tokens.shape[1] * width,
        "query_norm",
    )
    halo_own = permute(par, lambda n: n + 2 - 4 * (n % 2))
    halo_par = permute(own, lambda n: n - 2 + 4 * (n % 2))
    stat, near = call(
        functools.partial(near_kernel, count),
        [((4 * half, rows), F32), ((half, dim, 2 * rows), F32)],
        [q, own, par, halo_own, halo_par],
        2 * 2 * rows * 3 * rows * width * 2,
        "near",
    )
    bits = list(range(1, (count - 1).bit_length()))
    swapped = list(bits)
    for i in range(0, len(bits) - 1, 2):
        swapped[i], swapped[i + 1] = bits[i + 1], bits[i]
    for step in range(len(bits)):
        def partner(n, step=step):
            return n ^ (1 << (swapped[step] if n % 2 else bits[step]))

        received = permute(msg, partner)
        if step < len(bits) - 1:
            sums, side, msg = call(
                combine_kernel, [sums_s, side_s, msg_s], [sums, side, received], 1000000, "slots_combine"
            )
    keep, send = call(
        far_kernel,
        [((width, rows), BF16), ((width, rows), BF16)],
        [sums, side, received, q, stat, near],
        2 * 2 * rows * slots * width * 2,
        "far",
    )
    swapped_half = permute(send, lambda n: n ^ 1)
    (mixed,) = call(
        mix_kernel,
        [((rows, w_out.shape[1]), BF16)],
        [keep, swapped_half, w_out],
        2 * rows * w_out.shape[0] * w_out.shape[1],
        "mix",
    )
    return mixed


def solution(mesh):
    in_specs = (P(AXES, None), P(), P(), P(), P(), P())
    return jax.shard_map(
        per_device, mesh=mesh, in_specs=in_specs, out_specs=P(AXES, None), check_vma=False
    )
```

```python
import functools

import jax
import jax.numpy as jnp
from jax import lax
from jax.experimental import pallas as pl
from jax.experimental.pallas import tpu as pltpu
from jax.sharding import PartitionSpec as P

AXES = ("ctxa", "ctxb")
SIDE = 16
WINDOW = 128
EPS = 1e-05
BF16 = jnp.bfloat16
F32 = jnp.float32
VMEM = pltpu.VMEM


def dot(a, b, ca=1, cb=0):
    return lax.dot_general(a, b, (((ca,), (cb,)), ((), ())), preferred_element_type=F32)


def split_side(side):
    high = side.astype(BF16)
    rest = side - high.astype(F32)
    mid = rest.astype(BF16)
    low = rest - mid.astype(F32)
    parts = [high.astype(F32), mid.astype(F32), low, jnp.zeros_like(side)]
    return jnp.concatenate(parts, axis=0).astype(BF16)


def joined_side(msg_ref, at, rows):
    parts = msg_ref[at:, :].astype(F32)
    return parts[:rows] + parts[rows : 2 * rows] + parts[2 * rows : 3 * rows]


def merge(side_ref, msg_ref, heads, feats):
    own, other = side_ref[...], joined_side(msg_ref, heads * feats, 2 * heads)
    top = jnp.maximum(own[:heads], other[:heads])
    a, b = jnp.exp(own[:heads] - top), jnp.exp(other[:heads] - top)
    return top, own[heads:] * a + other[heads:] * b, a, b


def merged_sums(sums_ref, msg_ref, h, a, b):
    feats = sums_ref.shape[1]
    other = msg_ref[h * feats : (h + 1) * feats, :].astype(F32)
    return sums_ref[h] * a[h : h + 1] + other * b[h : h + 1]


def project_kernel(own_ref, wq_all, wk_all, wv_all, ws_all, wq_ref, wk_ref, wv_ref, ws_ref, kv_ref, sems):
    width = wk_ref.shape[1]
    half = ws_ref.shape[0]
    core = lax.axis_index(AXES) % 2
    cols = pl.ds(pl.multiple_of(core * width, width), width)
    heads = pl.ds(core * half, half)
    copies = [
        pltpu.make_async_copy(wk_all.at[:, cols], wk_ref, sems.at[0]),
        pltpu.make_async_copy(wv_all.at[:, cols], wv_ref, sems.at[1]),
        pltpu.make_async_copy(ws_all.at[heads], ws_ref, sems.at[2]),
        pltpu.make_async_copy(wq_all.at[:, cols], wq_ref, sems.at[3]),
    ]
    for copy in copies:
        copy.start()
    copies[0].wait()
    kv_ref[:, :width] = dot(own_ref[...], wk_ref[...]).astype(BF16)
    copies[1].wait()
    kv_ref[:, width:] = dot(own_ref[...], wv_ref[...]).astype(BF16)
    copies[2].wait()
    copies[3].wait()


def slots_kernel(par_ref, kv_own_ref, wk_ref, wv_ref, ws_ref, sums_ref, side_ref, msg_ref, kv_ref):
    heads, dim, _ = ws_ref.shape
    width = heads * dim
    feats = 2 * dim
    key_par = dot(par_ref[...], wk_ref[...]).astype(BF16)
    value_par = dot(par_ref[...], wv_ref[...]).astype(BF16)
    key = jnp.concatenate([kv_own_ref[:, :width], key_par], axis=0)
    value = jnp.concatenate([kv_own_ref[:, width:], value_par], axis=0)
    key_t, value_t = key.T, value.T
    tops, totals = [], []
    for h in range(heads):
        cols = slice(h * dim, (h + 1) * dim)
        pair = jnp.concatenate([key_t[cols], value_t[cols]], axis=0)
        kv_ref[h] = pair
        logits = dot(key[:, cols], ws_ref[h])
        top = jnp.max(logits, axis=0, keepdims=True)
        weight = jnp.exp(logits - top)
        tops.append(top)
        totals.append(jnp.sum(weight, axis=0, keepdims=True))
        high = weight.astype(BF16)
        low = (weight - high.astype(F32)).astype(BF16)
        sums = dot(pair, high) + dot(pair, low)
        sums_ref[h] = sums
        msg_ref[h * feats : (h + 1) * feats, :] = sums.astype(BF16)
    side = jnp.concatenate(tops + totals, axis=0)
    side_ref[...] = side
    msg_ref[heads * feats :, :] = split_side(side)


def combine_kernel(sums_ref, side_ref, msg_ref, *rest):
    sums_out, side_out, msg_out = rest[-3:]
    heads, feats, _ = sums_ref.shape
    top, total, a, b = merge(side_ref, msg_ref, heads, feats)
    side = jnp.concatenate([top, total], axis=0)
    side_out[...] = side
    msg_out[heads * feats :, :] = split_side(side)
    for h in range(heads):
        sums = merged_sums(sums_ref, msg_ref, h, a, b)
        sums_out[h] = sums
        msg_out[h * feats : (h + 1) * feats, :] = sums.astype(BF16)


def layer_norm_rows(u):
    center = u - jnp.mean(u, axis=0, keepdims=True)
    spread = jnp.mean(center * center, axis=0, keepdims=True)
    return center * lax.rsqrt(spread + EPS)


def query_kernel(own_ref, par_ref, wq_ref, kv_ref, q_ref, own_out, par_out):
    heads, both, _ = kv_ref.shape
    dim = both // 2
    rows = own_ref.shape[0]
    tokens = jnp.concatenate([own_ref[...], par_ref[...]], axis=0)
    q_ref[...] = dot(tokens, wq_ref[...]).astype(BF16).T
    for h in range(heads):
        near = layer_norm_rows(kv_ref[h, :dim, :].astype(F32)).astype(BF16)
        own_out[h, :dim, :] = near[:, :rows]
        par_out[h, :dim, :] = near[:, rows:]
        own_out[h, dim:, :] = kv_ref[h, dim:, :rows]
        par_out[h, dim:, :] = kv_ref[h, dim:, rows:]


def near_kernel(n_dev, q_ref, own_ref, par_ref, hown_ref, hpar_ref, _, stat_ref, out_ref):
    heads, both, rows = own_ref.shape
    dim = both // 2
    scale = 1.0 / dim**0.5
    me = lax.axis_index(AXES)
    core = me % 2
    u = lax.broadcasted_iota(jnp.int32, (rows, rows), 0)
    t = lax.broadcasted_iota(jnp.int32, (rows, rows), 1)
    flip = 1 - 2 * core
    before = (u - t) * flip >= 0
    after = (u - t) * flip <= 0
    has_own = jnp.where(core == 0, me >= 2, me < n_dev - 2)
    has_par = jnp.where(core == 0, me < n_dev - 2, me >= 2)
    ninf = -1e30
    for h in range(heads):
        for part in range(2):
            mine, other, halo = (own_ref, par_ref, hown_ref) if part == 0 else (par_ref, own_ref, hpar_ref)
            q = q_ref[h * dim : (h + 1) * dim, part * rows : (part + 1) * rows]
            s0 = dot(mine[h, :dim, :], q, 0, 0) * scale
            s1 = dot(other[h, :dim, :], q, 0, 0) * scale
            s2 = dot(halo[h, :dim, :], q, 0, 0) * scale
            if part == 0:
                s1 = jnp.where(after, s1, ninf)
                s2 = jnp.where(before & has_own, s2, ninf)
            else:
                s1 = jnp.where(before, s1, ninf)
                s2 = jnp.where(after & has_par, s2, ninf)
            top = jnp.max(jnp.maximum(jnp.maximum(s0, s1), s2), axis=0, keepdims=True)
            e0, e1, e2 = jnp.exp(s0 - top), jnp.exp(s1 - top), jnp.exp(s2 - top)
            total = jnp.sum(e0 + e1 + e2, axis=0, keepdims=True)
            out = (
                dot(mine[h, dim:, :], e0.astype(BF16))
                + dot(other[h, dim:, :], e1.astype(BF16))
                + dot(halo[h, dim:, :], e2.astype(BF16))
            )
            stat_ref[part, h : h + 1, :] = top
            stat_ref[part, heads + h : heads + h + 1, :] = total
            out_ref[part, h * dim : (h + 1) * dim, :] = out


def far_rows(part, h, keys, values, q_ref, stat_ref, near_ref):
    dim = keys.shape[0]
    heads = stat_ref.shape[1] // 2
    rows = near_ref.shape[2]
    q = q_ref[h * dim : (h + 1) * dim, part * rows : (part + 1) * rows]
    far = dot(keys, q, 0, 0) * (1.0 / dim**0.5)
    near_top = stat_ref[part, h : h + 1, :]
    near_total = stat_ref[part, heads + h : heads + h + 1, :]
    top = jnp.maximum(jnp.max(far, axis=0, keepdims=True), near_top)
    near_scale = jnp.exp(near_top - top)
    e = jnp.exp(far - top)
    denom = jnp.sum(e, axis=0, keepdims=True) + near_total * near_scale
    out = near_ref[part, h * dim : (h + 1) * dim, :] * near_scale + dot(values, e.astype(BF16))
    return (out / denom).astype(BF16)


def far_partner_kernel(sums_ref, side_ref, msg_ref, q_ref, stat_ref, near_ref, send_ref, slots_ref):
    heads, feats, _ = sums_ref.shape
    dim = feats // 2
    _, total, a, b = merge(side_ref, msg_ref, heads, feats)
    for h in range(heads):
        sums = merged_sums(sums_ref, msg_ref, h, a, b)
        keys = layer_norm_rows(sums[:dim]).astype(BF16)
        values = (sums[dim:] / total[h : h + 1]).astype(BF16)
        slots_ref[h, :dim, :] = keys
        slots_ref[h, dim:, :] = values
        send_ref[h * dim : (h + 1) * dim, :] = far_rows(1, h, keys, values, q_ref, stat_ref, near_ref)


def far_own_kernel(slots_ref, q_ref, stat_ref, near_ref, w_ref, out_ref):
    heads, feats, _ = slots_ref.shape
    dim = feats // 2
    width = heads * dim
    core = lax.axis_index(AXES) % 2
    rows = [
        far_rows(0, h, slots_ref[h, :dim, :], slots_ref[h, dim:, :], q_ref, stat_ref, near_ref)
        for h in range(heads)
    ]
    mine = pl.ds(pl.multiple_of(core * width, width), width)
    out_ref[...] = dot(jnp.concatenate(rows, axis=0), w_ref[mine, :], 0, 0)


def mix_kernel(part_ref, other_ref, w_ref, out_ref):
    width = other_ref.shape[0]
    core = lax.axis_index(AXES) % 2
    theirs = pl.ds(pl.multiple_of((1 - core) * width, width), width)
    out_ref[...] = (part_ref[...] + dot(other_ref[...], w_ref[theirs, :], 0, 0)).astype(BF16)


def call(kernel, outs, ins, flops, name, hbm=(), sems=0):
    spec = pl.BlockSpec(memory_space=VMEM)
    anywhere = pl.BlockSpec(memory_space=pl.ANY)
    out_shape = [jax.ShapeDtypeStruct(s, d) for s, d in outs]
    size = sum(x.size * x.dtype.itemsize for x in ins) + sum(
        s.size * s.dtype.itemsize for s in out_shape
    )
    return pl.pallas_call(
        kernel,
        out_shape=out_shape,
        in_specs=[anywhere if i in hbm else spec for i in range(len(ins))],
        out_specs=[spec] * len(outs),
        scratch_shapes=[pltpu.SemaphoreType.DMA((sems,))] if sems else [],
        compiler_params=pltpu.CompilerParams(vmem_limit_bytes=24 * 2**20),
        cost_estimate=pl.CostEstimate(flops=flops, bytes_accessed=size, transcendentals=0),
        name=name,
    )(*ins)


def per_device(tokens, w_query, w_key, w_value, w_slot, w_out):
    rows, model = tokens.shape
    count = lax.axis_size(AXES)
    heads, dim, slots = w_slot.shape
    half = heads // 2
    width = half * dim
    feats = 2 * dim

    def permute(x, target):
        pairs = [(n, target(n)) for n in range(count) if 0 <= target(n) < count]
        return lax.ppermute(x, AXES, pairs)

    weight_s = ((model, width), BF16)
    sums_s, side_s = ((half, feats, slots), F32), ((2 * half, slots), F32)
    msg_s = ((half * feats + 8 * half, slots), BF16)
    chunk_s = ((half, feats, rows), BF16)
    stat_s, near_s = ((2, 2 * half, rows), F32), ((2, width, rows), F32)

    other = permute(tokens, lambda n: n ^ 1)
    wq, wk, wv, ws, kv_own = call(
        project_kernel,
        [weight_s, weight_s, weight_s, ((half, dim, slots), BF16), ((rows, 2 * width), BF16)],
        [tokens, w_query, w_key, w_value, w_slot],
        2 * rows * model * width * 2,
        "project_own",
        hbm=(1, 2, 3, 4),
        sems=4,
    )
    sums, side, msg, kv = call(
        slots_kernel,
        [sums_s, side_s, msg_s, ((half, feats, 2 * rows), BF16)],
        [other, kv_own, wk, wv, ws],
        2 * rows * model * width * 2,
        "slots_local",
    )
    q, own, par = call(
        query_kernel,
        [((width, 2 * rows), BF16), chunk_s, chunk_s],
        [tokens, other, wq, kv],
        2 * 2 * rows * model * width,
        "query_norm",
    )
    halo_own = permute(par, lambda n: n + 2 - 4 * (n % 2))
    halo_par = permute(own, lambda n: n - 2 + 4 * (n % 2))
    bits = list(range(1, (count - 1).bit_length()))
    swapped = list(bits)
    for i in range(0, len(bits) - 1, 2):
        swapped[i], swapped[i + 1] = bits[i + 1], bits[i]
    for step in range(len(bits)):
        def partner(n, step=step):
            return n ^ (1 << (swapped[step] if n % 2 else bits[step]))

        received = permute(msg, partner)
        if step < len(bits) - 1:
            tied = [own] if step == 0 else []
            sums, side, msg = call(
                combine_kernel,
                [sums_s, side_s, msg_s],
                [sums, side, received] + tied,
                1000000,
                "slots_combine",
                hbm=(3,),
            )
    stat, near = call(
        functools.partial(near_kernel, count),
        [stat_s, near_s],
        [q, own, par, halo_own, halo_par, side],
        2 * 2 * rows * 3 * rows * width * 2,
        "near",
        hbm=(5,),
    )
    send, slot_kv = call(
        far_partner_kernel,
        [((width, rows), BF16), ((half, feats, slots), BF16)],
        [sums, side, received, q, stat, near],
        2 * rows * slots * width * 2,
        "far_partner",
    )
    (part,) = call(
        far_own_kernel,
        [((rows, w_out.shape[1]), F32)],
        [slot_kv, q, stat, near, w_out],
        2 * rows * slots * width * 2,
        "far_own",
    )
    their_half = permute(send, lambda n: n ^ 1)
    (mixed,) = call(
        mix_kernel,
        [((rows, w_out.shape[1]), BF16)],
        [part, their_half, w_out],
        2 * rows * width * w_out.shape[1],
        "mix",
    )
    return mixed


def solution(mesh):
    in_specs = (P(AXES, None), P(), P(), P(), P(), P())
    return jax.shard_map(
        per_device, mesh=mesh, in_specs=in_specs, out_specs=P(AXES, None), check_vma=False
    )
```

```python
import functools

import jax
import jax.numpy as jnp
from jax import lax
from jax.experimental import pallas as pl
from jax.experimental.pallas import tpu as pltpu
from jax.sharding import PartitionSpec as P

AXES = ("ctxa", "ctxb")
SIDE = 16
WINDOW = 128
EPS = 1e-05
BF16 = jnp.bfloat16
F32 = jnp.float32
VMEM = pltpu.VMEM


def dot(a, b, ca=1, cb=0):
    return lax.dot_general(a, b, (((ca,), (cb,)), ((), ())), preferred_element_type=F32)


def split_side(side):
    high = side.astype(BF16)
    rest = side - high.astype(F32)
    mid = rest.astype(BF16)
    low = rest - mid.astype(F32)
    parts = [high.astype(F32), mid.astype(F32), low, jnp.zeros_like(side)]
    return jnp.concatenate(parts, axis=0).astype(BF16)


def joined_side(msg_ref, at, rows):
    parts = msg_ref[at:, :].astype(F32)
    return parts[:rows] + parts[rows : 2 * rows] + parts[2 * rows : 3 * rows]


def merge(side_ref, msg_ref, heads, feats):
    own, other = side_ref[...], joined_side(msg_ref, heads * feats, 2 * heads)
    top = jnp.maximum(own[:heads], other[:heads])
    a, b = jnp.exp(own[:heads] - top), jnp.exp(other[:heads] - top)
    return top, own[heads:] * a + other[heads:] * b, a, b


def merged_sums(sums_ref, msg_ref, h, a, b):
    feats = sums_ref.shape[1]
    other = msg_ref[h * feats : (h + 1) * feats, :].astype(F32)
    return sums_ref[h] * a[h : h + 1] + other * b[h : h + 1]


def load_kernel(wq_all, wk_all, wv_all, wq_ref, wk_ref, wv_ref, sems):
    width = wk_ref.shape[1]
    core = lax.axis_index(AXES) % 2
    cols = pl.ds(pl.multiple_of(core * width, width), width)
    copies = [
        pltpu.make_async_copy(wk_all.at[:, cols], wk_ref, sems.at[0]),
        pltpu.make_async_copy(wv_all.at[:, cols], wv_ref, sems.at[1]),
        pltpu.make_async_copy(wq_all.at[:, cols], wq_ref, sems.at[2]),
    ]
    for copy in copies:
        copy.start()
    for copy in copies:
        copy.wait()


def slots_kernel(own_ref, par_ref, wk_ref, wv_ref, ws_ref, sums_ref, side_ref, msg_ref, kv_ref):
    heads, feats, _ = kv_ref.shape
    dim = feats // 2
    first = lax.axis_index(AXES) % 2 * heads
    tokens = jnp.concatenate([own_ref[...], par_ref[...]], axis=0)
    key = dot(tokens, wk_ref[...]).astype(BF16)
    value = dot(tokens, wv_ref[...]).astype(BF16)
    key_t, value_t = key.T, value.T
    tops, totals = [], []
    for h in range(heads):
        cols = slice(h * dim, (h + 1) * dim)
        pair = jnp.concatenate([key_t[cols], value_t[cols]], axis=0)
        kv_ref[h] = pair
        logits = dot(key[:, cols], ws_ref[first + h])
        top = jnp.max(logits, axis=0, keepdims=True)
        weight = jnp.exp(logits - top)
        tops.append(top)
        totals.append(jnp.sum(weight, axis=0, keepdims=True))
        high = weight.astype(BF16)
        low = (weight - high.astype(F32)).astype(BF16)
        sums = dot(pair, high) + dot(pair, low)
        sums_ref[h] = sums
        msg_ref[h * feats : (h + 1) * feats, :] = sums.astype(BF16)
    side = jnp.concatenate(tops + totals, axis=0)
    side_ref[...] = side
    msg_ref[heads * feats :, :] = split_side(side)


def combine_kernel(sums_ref, side_ref, msg_ref, *rest):
    sums_out, side_out, msg_out = rest[-3:]
    heads, feats, _ = sums_ref.shape
    top, total, a, b = merge(side_ref, msg_ref, heads, feats)
    side = jnp.concatenate([top, total], axis=0)
    side_out[...] = side
    msg_out[heads * feats :, :] = split_side(side)
    for h in range(heads):
        sums = merged_sums(sums_ref, msg_ref, h, a, b)
        sums_out[h] = sums
        msg_out[h * feats : (h + 1) * feats, :] = sums.astype(BF16)


def layer_norm_rows(u):
    center = u - jnp.mean(u, axis=0, keepdims=True)
    spread = jnp.mean(center * center, axis=0, keepdims=True)
    return center * lax.rsqrt(spread + EPS)


def query_kernel(own_ref, par_ref, wq_ref, kv_ref, q_ref, near_ref):
    heads, both, _ = kv_ref.shape
    dim = both // 2
    tokens = jnp.concatenate([own_ref[...], par_ref[...]], axis=0)
    q_ref[...] = dot(tokens, wq_ref[...]).astype(BF16).T
    for h in range(heads):
        near_ref[h, :dim, :] = layer_norm_rows(kv_ref[h, :dim, :].astype(F32)).astype(BF16)
        near_ref[h, dim:, :] = kv_ref[h, dim:, :]


def sides(rows):
    core = lax.axis_index(AXES) % 2
    u = lax.broadcasted_iota(jnp.int32, (rows, rows), 0)
    t = lax.broadcasted_iota(jnp.int32, (rows, rows), 1)
    ahead = (u - t) * (1 - 2 * core)
    return ahead >= 0, ahead <= 0


def chip_kernel(q_ref, kv_ref, _, stat_ref, out_ref):
    heads, both, span = kv_ref.shape
    rows = span // 2
    dim = both // 2
    scale = 1.0 / dim**0.5
    before, after = sides(rows)
    for h in range(heads):
        scores = dot(kv_ref[h, :dim, :], q_ref[h * dim : (h + 1) * dim, :], 0, 0) * scale
        for part in range(2):
            cols = slice(part * rows, (part + 1) * rows)
            s0, s1 = scores[:rows, cols], scores[rows:, cols]
            if part == 0:
                s1 = jnp.where(after, s1, -1e30)
            else:
                s0 = jnp.where(before, s0, -1e30)
            top = jnp.max(jnp.maximum(s0, s1), axis=0, keepdims=True)
            e0, e1 = jnp.exp(s0 - top), jnp.exp(s1 - top)
            e = jnp.concatenate([e0.astype(BF16), e1.astype(BF16)], axis=0)
            stat_ref[part, h : h + 1, :] = top
            stat_ref[part, heads + h : heads + h + 1, :] = jnp.sum(e0 + e1, axis=0, keepdims=True)
            out_ref[part, h * dim : (h + 1) * dim, :] = dot(kv_ref[h, dim:, :], e)


def halo_kernel(n_dev, hown_ref, hpar_ref, wk_ref, wv_ref, q_ref, chip_stat, chip_out, _, stat_ref, out_ref):
    rows = hown_ref.shape[0]
    width = wk_ref.shape[1]
    heads = stat_ref.shape[1] // 2
    dim = width // heads
    scale = 1.0 / dim**0.5
    tokens = jnp.concatenate([hown_ref[...], hpar_ref[...]], axis=0)
    key_t = dot(tokens, wk_ref[...]).astype(BF16).T
    value_t = dot(tokens, wv_ref[...]).astype(BF16).T
    me = lax.axis_index(AXES)
    first, last = me >= 2, me < n_dev - 2
    even = me % 2 == 0
    before, after = sides(rows)
    valid = [
        before & ((even & first) | (~even & last)),
        after & ((even & last) | (~even & first)),
    ]
    for h in range(heads):
        feats = slice(h * dim, (h + 1) * dim)
        near_keys = layer_norm_rows(key_t[feats].astype(F32)).astype(BF16)
        for part in range(2):
            cols = slice(part * rows, (part + 1) * rows)
            s = dot(near_keys[:, cols], q_ref[feats, cols], 0, 0) * scale
            s = jnp.where(valid[part], s, -1e30)
            old_top = chip_stat[part, h : h + 1, :]
            top = jnp.maximum(jnp.max(s, axis=0, keepdims=True), old_top)
            old_scale = jnp.exp(old_top - top)
            e = jnp.exp(s - top)
            stat_ref[part, h : h + 1, :] = top
            total = chip_stat[part, heads + h : heads + h + 1, :] * old_scale
            stat_ref[part, heads + h : heads + h + 1, :] = total + jnp.sum(e, axis=0, keepdims=True)
            out_ref[part, feats, :] = chip_out[part, feats, :] * old_scale + dot(
                value_t[feats, cols], e.astype(BF16)
            )


def far_rows(part, h, keys, values, q_ref, stat_ref, near_ref):
    dim = keys.shape[0]
    heads = stat_ref.shape[1] // 2
    rows = near_ref.shape[2]
    q = q_ref[h * dim : (h + 1) * dim, part * rows : (part + 1) * rows]
    far = dot(keys, q, 0, 0) * (1.0 / dim**0.5)
    near_top = stat_ref[part, h : h + 1, :]
    near_total = stat_ref[part, heads + h : heads + h + 1, :]
    top = jnp.maximum(jnp.max(far, axis=0, keepdims=True), near_top)
    near_scale = jnp.exp(near_top - top)
    e = jnp.exp(far - top)
    denom = jnp.sum(e, axis=0, keepdims=True) + near_total * near_scale
    out = near_ref[part, h * dim : (h + 1) * dim, :] * near_scale + dot(values, e.astype(BF16))
    return (out / denom).astype(BF16)


def far_partner_kernel(sums_ref, side_ref, msg_ref, q_ref, stat_ref, near_ref, send_ref, slots_ref):
    heads, feats, _ = sums_ref.shape
    dim = feats // 2
    _, total, a, b = merge(side_ref, msg_ref, heads, feats)
    for h in range(heads):
        sums = merged_sums(sums_ref, msg_ref, h, a, b)
        keys = layer_norm_rows(sums[:dim]).astype(BF16)
        values = (sums[dim:] / total[h : h + 1]).astype(BF16)
        slots_ref[h, :dim, :] = keys
        slots_ref[h, dim:, :] = values
        send_ref[h * dim : (h + 1) * dim, :] = far_rows(1, h, keys, values, q_ref, stat_ref, near_ref)


def far_own_kernel(slots_ref, q_ref, stat_ref, near_ref, w_ref, out_ref):
    heads, feats, _ = slots_ref.shape
    dim = feats // 2
    width = heads * dim
    core = lax.axis_index(AXES) % 2
    rows = [
        far_rows(0, h, slots_ref[h, :dim, :], slots_ref[h, dim:, :], q_ref, stat_ref, near_ref)
        for h in range(heads)
    ]
    mine = pl.ds(pl.multiple_of(core * width, width), width)
    out_ref[...] = dot(jnp.concatenate(rows, axis=0), w_ref[mine, :], 0, 0)


def mix_kernel(part_ref, other_ref, w_ref, out_ref):
    width = other_ref.shape[0]
    core = lax.axis_index(AXES) % 2
    theirs = pl.ds(pl.multiple_of((1 - core) * width, width), width)
    out_ref[...] = (part_ref[...] + dot(other_ref[...], w_ref[theirs, :], 0, 0)).astype(BF16)


def call(kernel, outs, ins, flops, name, unread=(), hbm=(), sems=0, grant=24):
    spec = pl.BlockSpec(memory_space=VMEM)
    anywhere = pl.BlockSpec(memory_space=pl.ANY)
    held = pl.BlockSpec(memory_space=pltpu.HBM)
    out_shape = [jax.ShapeDtypeStruct(s, d) for s, d in outs]
    size = sum(x.size * x.dtype.itemsize for x in ins) + sum(
        s.size * s.dtype.itemsize for s in out_shape
    )
    return pl.pallas_call(
        kernel,
        out_shape=out_shape,
        in_specs=[anywhere if i in unread else held if i in hbm else spec for i in range(len(ins))],
        out_specs=[spec] * len(outs),
        scratch_shapes=[pltpu.SemaphoreType.DMA((sems,))] if sems else [],
        compiler_params=pltpu.CompilerParams(vmem_limit_bytes=grant * 2**20),
        cost_estimate=pl.CostEstimate(flops=flops, bytes_accessed=size, transcendentals=0),
        name=name,
    )(*ins)


def per_device(tokens, w_query, w_key, w_value, w_slot, w_out):
    rows, model = tokens.shape
    count = lax.axis_size(AXES)
    heads, dim, slots = w_slot.shape
    half = heads // 2
    width = half * dim
    feats = 2 * dim

    def permute(x, target):
        pairs = [(n, target(n)) for n in range(count) if 0 <= target(n) < count]
        return lax.ppermute(x, AXES, pairs)

    weight_s = ((model, width), BF16)
    sums_s, side_s = ((half, feats, slots), F32), ((2 * half, slots), F32)
    msg_s = ((half * feats + 8 * half, slots), BF16)
    chunk_s = ((half, feats, rows), BF16)
    stat_s, near_s = ((2, 2 * half, rows), F32), ((2, width, rows), F32)

    other = permute(tokens, lambda n: n ^ 1)
    wq, wk, wv = call(
        load_kernel,
        [weight_s, weight_s, weight_s],
        [w_query, w_key, w_value],
        0,
        "load",
        hbm=(0, 1, 2),
        sems=3,
        grant=52,
    )
    sums, side, msg, kv = call(
        slots_kernel,
        [sums_s, side_s, msg_s, ((half, feats, 2 * rows), BF16)],
        [tokens, other, wk, wv, w_slot],
        2 * 2 * rows * model * width * 2,
        "slots_local",
    )
    q, near_kv = call(
        query_kernel,
        [((width, 2 * rows), BF16), ((half, feats, 2 * rows), BF16)],
        [tokens, other, wq, kv],
        2 * 2 * rows * model * width,
        "query_norm",
    )
    halo_own = permute(tokens, lambda n: n - 1 + 2 * (n % 2))
    bits = list(range(1, (count - 1).bit_length()))
    swapped = list(bits)
    for i in range(0, len(bits) - 1, 2):
        swapped[i], swapped[i + 1] = bits[i + 1], bits[i]
    def near_chip(side):
        return call(
            chip_kernel,
            [stat_s, near_s],
            [q, near_kv, side],
            2 * 2 * rows * 2 * rows * width * 2,
            "near_chip",
            unread=(2,),
        )

    steps = len(bits)
    tied = {1: [q]}
    if steps < 3:
        stat, near = near_chip(side)
    for step in range(steps):
        def partner(n, step=step):
            return n ^ (1 << (swapped[step] if n % 2 else bits[step]))

        received = permute(msg, partner)
        if step < steps - 1:
            sums, side, msg = call(
                combine_kernel,
                [sums_s, side_s, msg_s],
                [sums, side, received] + tied.get(step, []),
                1000000,
                "slots_combine",
                unread=(3,),
            )
        if step == steps - 3:
            halo_own, side = lax.optimization_barrier((halo_own, side))
            stat, near = near_chip(side)
            tied[steps - 2] = [stat]
    halo_par = permute(halo_own, lambda n: n ^ 1)
    stat, near = call(
        functools.partial(halo_kernel, count),
        [stat_s, near_s],
        [halo_own, halo_par, wk, wv, q, stat, near, side],
        2 * 2 * rows * model * width * 2,
        "near_halo",
        unread=(7,),
    )
    send, slot_kv = call(
        far_partner_kernel,
        [((width, rows), BF16), ((half, feats, slots), BF16)],
        [sums, side, received, q, stat, near],
        2 * rows * slots * width * 2,
        "far_partner",
    )
    (part,) = call(
        far_own_kernel,
        [((rows, w_out.shape[1]), F32)],
        [slot_kv, q, stat, near, w_out],
        2 * rows * slots * width * 2,
        "far_own",
    )
    their_half = permute(send, lambda n: n ^ 1)
    (mixed,) = call(
        mix_kernel,
        [((rows, w_out.shape[1]), BF16)],
        [part, their_half, w_out],
        2 * rows * width * w_out.shape[1],
        "mix",
    )
    return mixed


def solution(mesh):
    in_specs = (P(AXES, None), P(), P(), P(), P(), P())
    return jax.shard_map(
        per_device, mesh=mesh, in_specs=in_specs, out_specs=P(AXES, None), check_vma=False
    )
```

```python
import functools

import jax
import jax.numpy as jnp
from jax import lax
from jax.experimental import pallas as pl
from jax.experimental.pallas import tpu as pltpu
from jax.sharding import PartitionSpec as P

AXES = ("ctxa", "ctxb")
SIDE = 16
WINDOW = 128
EPS = 1e-05
BF16 = jnp.bfloat16
F32 = jnp.float32
VMEM = pltpu.VMEM


def dot(a, b, ca=1, cb=0):
    return lax.dot_general(a, b, (((ca,), (cb,)), ((), ())), preferred_element_type=F32)


def split_side(side):
    high = side.astype(BF16)
    rest = side - high.astype(F32)
    mid = rest.astype(BF16)
    low = rest - mid.astype(F32)
    parts = [high.astype(F32), mid.astype(F32), low, jnp.zeros_like(side)]
    return jnp.concatenate(parts, axis=0).astype(BF16)


def joined_side(msg_ref, at, rows):
    parts = msg_ref[at:, :].astype(F32)
    return parts[:rows] + parts[rows : 2 * rows] + parts[2 * rows : 3 * rows]


def merge(side_ref, msg_ref, heads, feats):
    own, other = side_ref[...], joined_side(msg_ref, heads * feats, 2 * heads)
    top = jnp.maximum(own[:heads], other[:heads])
    a, b = jnp.exp(own[:heads] - top), jnp.exp(other[:heads] - top)
    return top, own[heads:] * a + other[heads:] * b, a, b


def merged_sums(sums_ref, msg_ref, h, a, b):
    feats = sums_ref.shape[1]
    other = msg_ref[h * feats : (h + 1) * feats, :].astype(F32)
    return sums_ref[h] * a[h : h + 1] + other * b[h : h + 1]


def load_kernel(wq_all, wk_all, wv_all, wq_ref, wk_ref, wv_ref, sems):
    width = wk_ref.shape[1]
    core = lax.axis_index(AXES) % 2
    cols = pl.ds(pl.multiple_of(core * width, width), width)
    copies = [
        pltpu.make_async_copy(wk_all.at[:, cols], wk_ref, sems.at[0]),
        pltpu.make_async_copy(wv_all.at[:, cols], wv_ref, sems.at[1]),
        pltpu.make_async_copy(wq_all.at[:, cols], wq_ref, sems.at[2]),
    ]
    for copy in copies:
        copy.start()
    for copy in copies:
        copy.wait()


def slots_kernel(own_ref, par_ref, wk_ref, wv_ref, ws_ref, sums_ref, side_ref, msg_ref, kv_ref):
    heads, feats, _ = kv_ref.shape
    dim = feats // 2
    first = lax.axis_index(AXES) % 2 * heads
    tokens = jnp.concatenate([own_ref[...], par_ref[...]], axis=0)
    key = dot(tokens, wk_ref[...]).astype(BF16)
    value = dot(tokens, wv_ref[...]).astype(BF16)
    key_t, value_t = key.T, value.T
    tops, totals = [], []
    for h in range(heads):
        cols = slice(h * dim, (h + 1) * dim)
        pair = jnp.concatenate([key_t[cols], value_t[cols]], axis=0)
        kv_ref[h] = pair
        logits = dot(key[:, cols], ws_ref[first + h])
        top = jnp.max(logits, axis=0, keepdims=True)
        weight = jnp.exp(logits - top)
        tops.append(top)
        totals.append(jnp.sum(weight, axis=0, keepdims=True))
        high = weight.astype(BF16)
        low = (weight - high.astype(F32)).astype(BF16)
        sums = dot(pair, high) + dot(pair, low)
        sums_ref[h] = sums
        msg_ref[h * feats : (h + 1) * feats, :] = sums.astype(BF16)
    side = jnp.concatenate(tops + totals, axis=0)
    side_ref[...] = side
    msg_ref[heads * feats :, :] = split_side(side)


def combine_kernel(sums_ref, side_ref, msg_ref, *rest):
    sums_out, side_out, msg_out = rest[-3:]
    heads, feats, _ = sums_ref.shape
    top, total, a, b = merge(side_ref, msg_ref, heads, feats)
    side = jnp.concatenate([top, total], axis=0)
    side_out[...] = side
    msg_out[heads * feats :, :] = split_side(side)
    for h in range(heads):
        sums = merged_sums(sums_ref, msg_ref, h, a, b)
        sums_out[h] = sums
        msg_out[h * feats : (h + 1) * feats, :] = sums.astype(BF16)


def layer_norm_rows(u):
    center = u - jnp.mean(u, axis=0, keepdims=True)
    spread = jnp.mean(center * center, axis=0, keepdims=True)
    return center * lax.rsqrt(spread + EPS)


def query_kernel(own_ref, par_ref, wq_ref, kv_ref, q_ref, near_ref):
    heads, both, _ = kv_ref.shape
    dim = both // 2
    tokens = jnp.concatenate([own_ref[...], par_ref[...]], axis=0)
    q_ref[...] = dot(tokens, wq_ref[...]).astype(BF16).T
    for h in range(heads):
        near_ref[h, :dim, :] = layer_norm_rows(kv_ref[h, :dim, :].astype(F32)).astype(BF16)
        near_ref[h, dim:, :] = kv_ref[h, dim:, :]


def sides(rows):
    core = lax.axis_index(AXES) % 2
    u = lax.broadcasted_iota(jnp.int32, (rows, rows), 0)
    t = lax.broadcasted_iota(jnp.int32, (rows, rows), 1)
    ahead = (u - t) * (1 - 2 * core)
    return ahead >= 0, ahead <= 0


def chip_kernel(q_ref, kv_ref, _, stat_ref, out_ref):
    heads, both, span = kv_ref.shape
    rows = span // 2
    dim = both // 2
    scale = 1.0 / dim**0.5
    before, after = sides(rows)
    for h in range(heads):
        scores = dot(kv_ref[h, :dim, :], q_ref[h * dim : (h + 1) * dim, :], 0, 0) * scale
        for part in range(2):
            cols = slice(part * rows, (part + 1) * rows)
            s0, s1 = scores[:rows, cols], scores[rows:, cols]
            if part == 0:
                s1 = jnp.where(after, s1, -1e30)
            else:
                s0 = jnp.where(before, s0, -1e30)
            top = jnp.max(jnp.maximum(s0, s1), axis=0, keepdims=True)
            e0, e1 = jnp.exp(s0 - top), jnp.exp(s1 - top)
            e = jnp.concatenate([e0.astype(BF16), e1.astype(BF16)], axis=0)
            stat_ref[part, h : h + 1, :] = top
            stat_ref[part, heads + h : heads + h + 1, :] = jnp.sum(e0 + e1, axis=0, keepdims=True)
            out_ref[part, h * dim : (h + 1) * dim, :] = dot(kv_ref[h, dim:, :], e)


def halo_kernel(n_dev, hown_ref, hpar_ref, wk_ref, wv_ref, q_ref, chip_stat, chip_out, _, stat_ref, out_ref):
    rows = hown_ref.shape[0]
    width = wk_ref.shape[1]
    heads = stat_ref.shape[1] // 2
    dim = width // heads
    scale = 1.0 / dim**0.5
    tokens = jnp.concatenate([hown_ref[...], hpar_ref[...]], axis=0)
    key_t = dot(tokens, wk_ref[...]).astype(BF16).T
    value_t = dot(tokens, wv_ref[...]).astype(BF16).T
    me = lax.axis_index(AXES)
    first, last = me >= 2, me < n_dev - 2
    even = me % 2 == 0
    before, after = sides(rows)
    valid = [
        before & ((even & first) | (~even & last)),
        after & ((even & last) | (~even & first)),
    ]
    for h in range(heads):
        feats = slice(h * dim, (h + 1) * dim)
        near_keys = layer_norm_rows(key_t[feats].astype(F32)).astype(BF16)
        for part in range(2):
            cols = slice(part * rows, (part + 1) * rows)
            s = dot(near_keys[:, cols], q_ref[feats, cols], 0, 0) * scale
            s = jnp.where(valid[part], s, -1e30)
            old_top = chip_stat[part, h : h + 1, :]
            top = jnp.maximum(jnp.max(s, axis=0, keepdims=True), old_top)
            old_scale = jnp.exp(old_top - top)
            e = jnp.exp(s - top)
            stat_ref[part, h : h + 1, :] = top
            total = chip_stat[part, heads + h : heads + h + 1, :] * old_scale
            stat_ref[part, heads + h : heads + h + 1, :] = total + jnp.sum(e, axis=0, keepdims=True)
            out_ref[part, feats, :] = chip_out[part, feats, :] * old_scale + dot(
                value_t[feats, cols], e.astype(BF16)
            )


def far_rows(part, h, keys, values, q_ref, stat_ref, near_ref):
    dim = keys.shape[0]
    heads = stat_ref.shape[1] // 2
    rows = near_ref.shape[2]
    q = q_ref[h * dim : (h + 1) * dim, part * rows : (part + 1) * rows]
    far = dot(keys, q, 0, 0) * (1.0 / dim**0.5)
    near_top = stat_ref[part, h : h + 1, :]
    near_total = stat_ref[part, heads + h : heads + h + 1, :]
    top = jnp.maximum(jnp.max(far, axis=0, keepdims=True), near_top)
    near_scale = jnp.exp(near_top - top)
    e = jnp.exp(far - top)
    denom = jnp.sum(e, axis=0, keepdims=True) + near_total * near_scale
    out = near_ref[part, h * dim : (h + 1) * dim, :] * near_scale + dot(values, e.astype(BF16))
    return (out / denom).astype(BF16)


def far_partner_kernel(sums_ref, side_ref, msg_ref, q_ref, stat_ref, near_ref, send_ref, slots_ref):
    heads, feats, _ = sums_ref.shape
    dim = feats // 2
    _, total, a, b = merge(side_ref, msg_ref, heads, feats)
    for h in range(heads):
        sums = merged_sums(sums_ref, msg_ref, h, a, b)
        keys = layer_norm_rows(sums[:dim]).astype(BF16)
        values = (sums[dim:] / total[h : h + 1]).astype(BF16)
        slots_ref[h, :dim, :] = keys
        slots_ref[h, dim:, :] = values
        send_ref[h * dim : (h + 1) * dim, :] = far_rows(1, h, keys, values, q_ref, stat_ref, near_ref)


def far_own_kernel(slots_ref, q_ref, stat_ref, near_ref, w_ref, out_ref):
    heads, feats, _ = slots_ref.shape
    dim = feats // 2
    width = heads * dim
    core = lax.axis_index(AXES) % 2
    rows = [
        far_rows(0, h, slots_ref[h, :dim, :], slots_ref[h, dim:, :], q_ref, stat_ref, near_ref)
        for h in range(heads)
    ]
    mine = pl.ds(pl.multiple_of(core * width, width), width)
    out_ref[...] = dot(jnp.concatenate(rows, axis=0), w_ref[mine, :], 0, 0)


def mix_kernel(part_ref, other_ref, w_ref, out_ref, held_ref, sems):
    width = other_ref.shape[0]
    pieces = sems.shape[0]
    cols = out_ref.shape[1] // pieces
    core = lax.axis_index(AXES) % 2
    theirs = pl.ds(pl.multiple_of((1 - core) * width, width), width)
    other = other_ref[...].T
    copies = []
    for i in range(pieces):
        at = slice(i * cols, (i + 1) * cols)
        held_ref[:, at] = (part_ref[:, at] + dot(other, w_ref[theirs, at])).astype(BF16)
        copies.append(pltpu.make_async_copy(held_ref.at[:, at], out_ref.at[:, at], sems.at[i]))
        copies[i].start()
    for copy in copies:
        copy.wait()


def call(kernel, outs, ins, flops, name, unread=(), hbm=(), sems=0, grant=24, held=None):
    spec = pl.BlockSpec(memory_space=VMEM)
    anywhere = pl.BlockSpec(memory_space=pl.ANY)
    stays = pl.BlockSpec(memory_space=pltpu.HBM)
    out_shape = [jax.ShapeDtypeStruct(s, d) for s, d in outs]
    size = sum(x.size * x.dtype.itemsize for x in ins) + sum(
        s.size * s.dtype.itemsize for s in out_shape
    )
    return pl.pallas_call(
        kernel,
        out_shape=out_shape,
        in_specs=[anywhere if i in unread else stays if i in hbm else spec for i in range(len(ins))],
        out_specs=[stays if held else spec] * len(outs),
        scratch_shapes=([held] if held else []) + ([pltpu.SemaphoreType.DMA((sems,))] if sems else []),
        compiler_params=pltpu.CompilerParams(vmem_limit_bytes=grant * 2**20),
        cost_estimate=pl.CostEstimate(flops=flops, bytes_accessed=size, transcendentals=0),
        name=name,
    )(*ins)


def per_device(tokens, w_query, w_key, w_value, w_slot, w_out):
    rows, model = tokens.shape
    count = lax.axis_size(AXES)
    heads, dim, slots = w_slot.shape
    half = heads // 2
    width = half * dim
    feats = 2 * dim

    def permute(x, target):
        pairs = [(n, target(n)) for n in range(count) if 0 <= target(n) < count]
        return lax.ppermute(x, AXES, pairs)

    weight_s = ((model, width), BF16)
    sums_s, side_s = ((half, feats, slots), F32), ((2 * half, slots), F32)
    msg_s = ((half * feats + 8 * half, slots), BF16)
    chunk_s = ((half, feats, rows), BF16)
    stat_s, near_s = ((2, 2 * half, rows), F32), ((2, width, rows), F32)

    other = permute(tokens, lambda n: n ^ 1)
    wq, wk, wv = call(
        load_kernel,
        [weight_s, weight_s, weight_s],
        [w_query, w_key, w_value],
        0,
        "load",
        hbm=(0, 1, 2),
        sems=3,
        grant=52,
    )
    sums, side, msg, kv = call(
        slots_kernel,
        [sums_s, side_s, msg_s, ((half, feats, 2 * rows), BF16)],
        [tokens, other, wk, wv, w_slot],
        2 * 2 * rows * model * width * 2,
        "slots_local",
    )
    q, near_kv = call(
        query_kernel,
        [((width, 2 * rows), BF16), ((half, feats, 2 * rows), BF16)],
        [tokens, other, wq, kv],
        2 * 2 * rows * model * width,
        "query_norm",
    )
    halo_own = permute(tokens, lambda n: n - 1 + 2 * (n % 2))
    bits = list(range(1, (count - 1).bit_length()))
    half_bits = len(bits) // 2
    high, low = bits[half_bits:][::-1], bits[:half_bits][::-1]
    bits, swapped = [], []
    for i in range(len(high)):
        pair = high[i : i + 1] + low[i : i + 1]
        bits += pair
        swapped += pair[::-1]
    def near_chip(side):
        return call(
            chip_kernel,
            [stat_s, near_s],
            [q, near_kv, side],
            2 * 2 * rows * 2 * rows * width * 2,
            "near_chip",
            unread=(2,),
        )

    steps = len(bits)
    tied = {1: [q]}
    if steps < 3:
        stat, near = near_chip(side)
    for step in range(steps):
        def partner(n, step=step):
            return n ^ (1 << (swapped[step] if n % 2 else bits[step]))

        received = permute(msg, partner)
        if step < steps - 1:
            sums, side, msg = call(
                combine_kernel,
                [sums_s, side_s, msg_s],
                [sums, side, received] + tied.get(step, []),
                1000000,
                "slots_combine",
                unread=(3,),
            )
        if step == steps - 3:
            halo_own, side = lax.optimization_barrier((halo_own, side))
            stat, near = near_chip(side)
            tied[steps - 2] = [stat]
    halo_par = permute(halo_own, lambda n: n ^ 1)
    stat, near = call(
        functools.partial(halo_kernel, count),
        [stat_s, near_s],
        [halo_own, halo_par, wk, wv, q, stat, near, side],
        2 * 2 * rows * model * width * 2,
        "near_halo",
        unread=(7,),
    )
    send, slot_kv = call(
        far_partner_kernel,
        [((width, rows), BF16), ((half, feats, slots), BF16)],
        [sums, side, received, q, stat, near],
        2 * rows * slots * width * 2,
        "far_partner",
    )
    (part,) = call(
        far_own_kernel,
        [((rows, w_out.shape[1]), F32)],
        [slot_kv, q, stat, near, w_out],
        2 * rows * slots * width * 2,
        "far_own",
    )
    their_half = permute(send, lambda n: n ^ 1)
    (mixed,) = call(
        mix_kernel,
        [((rows, w_out.shape[1]), BF16)],
        [part, their_half, w_out],
        2 * rows * width * w_out.shape[1],
        "mix",
        sems=4,
        held=VMEM((rows, w_out.shape[1]), BF16),
    )
    return mixed


def solution(mesh):
    in_specs = (P(AXES, None), P(), P(), P(), P(), P())
    return jax.shard_map(
        per_device, mesh=mesh, in_specs=in_specs, out_specs=P(AXES, None), check_vma=False
    )
```

```python
import functools

import jax
import jax.numpy as jnp
from jax import lax
from jax.experimental import pallas as pl
from jax.experimental.pallas import tpu as pltpu
from jax.sharding import PartitionSpec as P

AXES = ("ctxa", "ctxb")
SIDE = 16
WINDOW = 128
EPS = 1e-05
BF16 = jnp.bfloat16
F32 = jnp.float32
VMEM = pltpu.VMEM


def dot(a, b, ca=1, cb=0):
    return lax.dot_general(a, b, (((ca,), (cb,)), ((), ())), preferred_element_type=F32)


def split_side(side):
    high = side.astype(BF16)
    rest = side - high.astype(F32)
    mid = rest.astype(BF16)
    low = rest - mid.astype(F32)
    parts = [high.astype(F32), mid.astype(F32), low, jnp.zeros_like(side)]
    return jnp.concatenate(parts, axis=0).astype(BF16)


def joined_side(msg_ref, at, rows):
    parts = msg_ref[at:, :].astype(F32)
    return parts[:rows] + parts[rows : 2 * rows] + parts[2 * rows : 3 * rows]


def merge(side_ref, msg_ref, heads, feats):
    own, other = side_ref[...], joined_side(msg_ref, heads * feats, 2 * heads)
    top = jnp.maximum(own[:heads], other[:heads])
    a, b = jnp.exp(own[:heads] - top), jnp.exp(other[:heads] - top)
    return top, own[heads:] * a + other[heads:] * b, a, b


def merged_sums(sums_ref, msg_ref, h, a, b):
    feats = sums_ref.shape[1]
    other = msg_ref[h * feats : (h + 1) * feats, :].astype(F32)
    return sums_ref[h] * a[h : h + 1] + other * b[h : h + 1]


def load_kernel(wk_all, wv_all, wk_ref, wv_ref, sems):
    width = wk_ref.shape[1]
    core = lax.axis_index(AXES) % 2
    cols = pl.ds(pl.multiple_of(core * width, width), width)
    copies = [
        pltpu.make_async_copy(wk_all.at[:, cols], wk_ref, sems.at[0]),
        pltpu.make_async_copy(wv_all.at[:, cols], wv_ref, sems.at[1]),
    ]
    for copy in copies:
        copy.start()
    for copy in copies:
        copy.wait()


def slots_kernel(own_ref, par_ref, wk_ref, wv_ref, ws_ref, sums_ref, side_ref, msg_ref, kv_ref):
    heads, feats, _ = kv_ref.shape
    dim = feats // 2
    first = lax.axis_index(AXES) % 2 * heads
    tokens = jnp.concatenate([own_ref[...], par_ref[...]], axis=0)
    key = dot(tokens, wk_ref[...]).astype(BF16)
    value = dot(tokens, wv_ref[...]).astype(BF16)
    key_t, value_t = key.T, value.T
    cols = [slice(h * dim, (h + 1) * dim) for h in range(heads)]
    logits = [dot(key[:, c], ws_ref[first + h]) for h, c in enumerate(cols)]
    pairs = [jnp.concatenate([key_t[c], value_t[c]], axis=0) for c in cols]
    tops = [jnp.max(x, axis=0, keepdims=True) for x in logits]
    weights = [jnp.exp(x - top) for x, top in zip(logits, tops)]
    totals = [jnp.sum(x, axis=0, keepdims=True) for x in weights]
    side = jnp.concatenate(tops + totals, axis=0)
    side_ref[...] = side
    msg_ref[heads * feats :, :] = split_side(side)
    for h in range(heads):
        kv_ref[h] = pairs[h]
        high = weights[h].astype(BF16)
        low = (weights[h] - high.astype(F32)).astype(BF16)
        both = dot(pairs[h], jnp.concatenate([high, low], axis=1))
        sums = both[:, : high.shape[1]] + both[:, high.shape[1] :]
        sums_ref[h] = sums
        msg_ref[h * feats : (h + 1) * feats, :] = sums.astype(BF16)


def combine_kernel(sums_ref, side_ref, msg_ref, *rest):
    sums_out, side_out, msg_out = rest[-3:]
    heads, feats, _ = sums_ref.shape
    top, total, a, b = merge(side_ref, msg_ref, heads, feats)
    side = jnp.concatenate([top, total], axis=0)
    side_out[...] = side
    msg_out[heads * feats :, :] = split_side(side)
    for h in range(heads):
        sums = merged_sums(sums_ref, msg_ref, h, a, b)
        sums_out[h] = sums
        msg_out[h * feats : (h + 1) * feats, :] = sums.astype(BF16)


def layer_norm_rows(u):
    center = u - jnp.mean(u, axis=0, keepdims=True)
    spread = jnp.mean(center * center, axis=0, keepdims=True)
    return center * lax.rsqrt(spread + EPS)


def query_kernel(own_ref, par_ref, wq_all, kv_ref, q_ref, near_ref, wq_ref, sems):
    width = wq_ref.shape[1]
    core = lax.axis_index(AXES) % 2
    cols = pl.ds(pl.multiple_of(core * width, width), width)
    copy = pltpu.make_async_copy(wq_all.at[:, cols], wq_ref, sems.at[0])
    copy.start()
    heads, both, _ = kv_ref.shape
    dim = both // 2
    near = [layer_norm_rows(kv_ref[h, :dim, :].astype(F32)).astype(BF16) for h in range(heads)]
    values = [kv_ref[h, dim:, :] for h in range(heads)]
    tokens = jnp.concatenate([own_ref[...], par_ref[...]], axis=0)
    copy.wait()
    q_ref[...] = dot(tokens, wq_ref[...]).astype(BF16).T
    for h in range(heads):
        near_ref[h, :dim, :] = near[h]
        near_ref[h, dim:, :] = values[h]


def sides(rows):
    core = lax.axis_index(AXES) % 2
    u = lax.broadcasted_iota(jnp.int32, (rows, rows), 0)
    t = lax.broadcasted_iota(jnp.int32, (rows, rows), 1)
    ahead = (u - t) * (1 - 2 * core)
    return ahead >= 0, ahead <= 0


def chip_kernel(q_ref, kv_ref, _, stat_ref, out_ref):
    heads, both, span = kv_ref.shape
    rows = span // 2
    dim = both // 2
    scale = 1.0 / dim**0.5
    before, after = sides(rows)
    scores = [
        dot(kv_ref[h, :dim, :], q_ref[h * dim : (h + 1) * dim, :], 0, 0) * scale
        for h in range(heads)
    ]
    items = [(h, part) for part in range(2) for h in range(heads)]
    halves = [
        (
            scores[h][:rows, :rows] if part == 0 else jnp.where(before, scores[h][:rows, rows:], -1e30),
            scores[h][rows:, rows:] if part == 1 else jnp.where(after, scores[h][rows:, :rows], -1e30),
        )
        for h, part in items
    ]
    tops = [jnp.max(jnp.maximum(s0, s1), axis=0, keepdims=True) for s0, s1 in halves]
    exps = [(jnp.exp(s0 - top), jnp.exp(s1 - top)) for (s0, s1), top in zip(halves, tops)]
    totals = [jnp.sum(e0 + e1, axis=0, keepdims=True) for e0, e1 in exps]
    wide = [jnp.concatenate([e0.astype(BF16), e1.astype(BF16)], axis=0) for e0, e1 in exps]
    outs = [
        dot(kv_ref[h, dim:, :], jnp.concatenate([wide[h], wide[heads + h]], axis=1))
        for h in range(heads)
    ]
    for part in range(2):
        of = slice(part * heads, (part + 1) * heads)
        stat_ref[part] = jnp.concatenate(tops[of] + totals[of], axis=0)
        out_ref[part] = jnp.concatenate([x[:, part * rows : (part + 1) * rows] for x in outs], axis=0)


def halo_kernel(n_dev, hown_ref, hpar_ref, wk_ref, wv_ref, q_ref, chip_stat, chip_out, _, stat_ref, out_ref):
    rows = hown_ref.shape[0]
    width = wk_ref.shape[1]
    heads = stat_ref.shape[1] // 2
    dim = width // heads
    scale = 1.0 / dim**0.5
    tokens = jnp.concatenate([hown_ref[...], hpar_ref[...]], axis=0)
    key_t = dot(tokens, wk_ref[...]).astype(BF16).T
    value_t = dot(tokens, wv_ref[...]).astype(BF16).T
    me = lax.axis_index(AXES)
    first, last = me >= 2, me < n_dev - 2
    even = me % 2 == 0
    before, after = sides(rows)
    valid = [
        before & ((even & first) | (~even & last)),
        after & ((even & last) | (~even & first)),
    ]
    feats = [slice(h * dim, (h + 1) * dim) for h in range(heads)]
    cols = [slice(part * rows, (part + 1) * rows) for part in range(2)]
    near_keys = [layer_norm_rows(key_t[f].astype(F32)).astype(BF16) for f in feats]
    items = [(h, part) for part in range(2) for h in range(heads)]
    scores = [
        jnp.where(
            valid[part], dot(near_keys[h][:, cols[part]], q_ref[feats[h], cols[part]], 0, 0) * scale, -1e30
        )
        for h, part in items
    ]
    old_tops = [chip_stat[part, h : h + 1, :] for h, part in items]
    tops = [jnp.maximum(jnp.max(s, axis=0, keepdims=True), t) for s, t in zip(scores, old_tops)]
    old_scales = [jnp.exp(t - top) for t, top in zip(old_tops, tops)]
    exps = [jnp.exp(s - top) for s, top in zip(scores, tops)]
    totals = [
        chip_stat[part, heads + h : heads + h + 1, :] * a + jnp.sum(e, axis=0, keepdims=True)
        for (h, part), a, e in zip(items, old_scales, exps)
    ]
    outs = [
        chip_out[part, feats[h], :] * a + dot(value_t[feats[h], cols[part]], e.astype(BF16))
        for (h, part), a, e in zip(items, old_scales, exps)
    ]
    for part in range(2):
        of = slice(part * heads, (part + 1) * heads)
        stat_ref[part] = jnp.concatenate(tops[of] + totals[of], axis=0)
        out_ref[part] = jnp.concatenate(outs[of], axis=0)


def far_rows(part, slots, q_ref, stat_ref, near_ref):
    heads = len(slots)
    dim = slots[0][0].shape[0]
    rows = near_ref.shape[2]
    feats = [slice(h * dim, (h + 1) * dim) for h in range(heads)]
    cols = slice(part * rows, (part + 1) * rows)
    scale = 1.0 / dim**0.5
    far = [dot(keys, q_ref[f, cols], 0, 0) * scale for (keys, _), f in zip(slots, feats)]
    near_tops = [stat_ref[part, h : h + 1, :] for h in range(heads)]
    tops = [jnp.maximum(jnp.max(x, axis=0, keepdims=True), t) for x, t in zip(far, near_tops)]
    near_scales = [jnp.exp(t - top) for t, top in zip(near_tops, tops)]
    exps = [jnp.exp(x - top) for x, top in zip(far, tops)]
    denoms = [
        jnp.sum(e, axis=0, keepdims=True) + stat_ref[part, heads + h : heads + h + 1, :] * near_scales[h]
        for h, e in enumerate(exps)
    ]
    outs = [
        near_ref[part, f, :] * a + dot(values, e.astype(BF16))
        for f, a, (_, values), e in zip(feats, near_scales, slots, exps)
    ]
    return jnp.concatenate([(x / d).astype(BF16) for x, d in zip(outs, denoms)], axis=0)


def far_partner_kernel(sums_ref, side_ref, msg_ref, q_ref, stat_ref, near_ref, send_ref, slots_ref):
    heads, feats, _ = sums_ref.shape
    dim = feats // 2
    _, total, a, b = merge(side_ref, msg_ref, heads, feats)
    sums = [merged_sums(sums_ref, msg_ref, h, a, b) for h in range(heads)]
    slots = [
        (layer_norm_rows(x[:dim]).astype(BF16), (x[dim:] / total[h : h + 1]).astype(BF16))
        for h, x in enumerate(sums)
    ]
    send_ref[...] = far_rows(1, slots, q_ref, stat_ref, near_ref)
    for h, (keys, values) in enumerate(slots):
        slots_ref[h, :dim, :] = keys
        slots_ref[h, dim:, :] = values


def far_own_kernel(slots_ref, q_ref, stat_ref, near_ref, w_ref, out_ref):
    heads, feats, _ = slots_ref.shape
    dim = feats // 2
    width = heads * dim
    core = lax.axis_index(AXES) % 2
    slots = [(slots_ref[h, :dim, :], slots_ref[h, dim:, :]) for h in range(heads)]
    rows = far_rows(0, slots, q_ref, stat_ref, near_ref)
    mine = pl.ds(pl.multiple_of(core * width, width), width)
    out_ref[...] = dot(rows, w_ref[mine, :], 0, 0)


def mix_kernel(part_ref, other_ref, w_ref, out_ref, held_ref, sems):
    width = other_ref.shape[0]
    pieces = sems.shape[0]
    cols = out_ref.shape[1] // pieces
    core = lax.axis_index(AXES) % 2
    theirs = pl.ds(pl.multiple_of((1 - core) * width, width), width)
    other = other_ref[...].T
    copies = []
    for i in range(pieces):
        at = slice(i * cols, (i + 1) * cols)
        held_ref[:, at] = (part_ref[:, at] + dot(other, w_ref[theirs, at])).astype(BF16)
        copies.append(pltpu.make_async_copy(held_ref.at[:, at], out_ref.at[:, at], sems.at[i]))
        copies[i].start()
    for copy in copies:
        copy.wait()


def call(kernel, outs, ins, flops, name, unread=(), hbm=(), sems=0, grant=24, held=None, scratch=None):
    spec = pl.BlockSpec(memory_space=VMEM)
    anywhere = pl.BlockSpec(memory_space=pl.ANY)
    stays = pl.BlockSpec(memory_space=pltpu.HBM)
    out_shape = [jax.ShapeDtypeStruct(s, d) for s, d in outs]
    size = sum(x.size * x.dtype.itemsize for x in ins) + sum(
        s.size * s.dtype.itemsize for s in out_shape
    )
    return pl.pallas_call(
        kernel,
        out_shape=out_shape,
        in_specs=[anywhere if i in unread else stays if i in hbm else spec for i in range(len(ins))],
        out_specs=[stays if held else spec] * len(outs),
        scratch_shapes=[x for x in (held, scratch) if x] + ([pltpu.SemaphoreType.DMA((sems,))] if sems else []),
        compiler_params=pltpu.CompilerParams(vmem_limit_bytes=grant * 2**20),
        cost_estimate=pl.CostEstimate(flops=flops, bytes_accessed=size, transcendentals=0),
        name=name,
    )(*ins)


def per_device(tokens, w_query, w_key, w_value, w_slot, w_out):
    rows, model = tokens.shape
    count = lax.axis_size(AXES)
    heads, dim, slots = w_slot.shape
    half = heads // 2
    width = half * dim
    feats = 2 * dim

    def permute(x, target):
        pairs = [(n, target(n)) for n in range(count) if 0 <= target(n) < count]
        return lax.ppermute(x, AXES, pairs)

    weight_s = ((model, width), BF16)
    sums_s, side_s = ((half, feats, slots), F32), ((2 * half, slots), F32)
    msg_s = ((half * feats + 8 * half, slots), BF16)
    chunk_s = ((half, feats, rows), BF16)
    stat_s, near_s = ((2, 2 * half, rows), F32), ((2, width, rows), F32)

    other = permute(tokens, lambda n: n ^ 1)
    wk, wv = call(
        load_kernel,
        [weight_s, weight_s],
        [w_key, w_value],
        0,
        "load",
        hbm=(0, 1),
        sems=2,
        grant=52,
    )
    sums, side, msg, kv = call(
        slots_kernel,
        [sums_s, side_s, msg_s, ((half, feats, 2 * rows), BF16)],
        [tokens, other, wk, wv, w_slot],
        2 * 2 * rows * model * width * 2,
        "slots_local",
    )
    q, near_kv = call(
        query_kernel,
        [((width, 2 * rows), BF16), ((half, feats, 2 * rows), BF16)],
        [tokens, other, w_query, kv],
        2 * 2 * rows * model * width,
        "query_norm",
        hbm=(2,),
        sems=1,
        scratch=VMEM((model, width), BF16),
    )
    halo_own = permute(tokens, lambda n: n - 1 + 2 * (n % 2))
    bits = list(range(1, (count - 1).bit_length()))
    half_bits = len(bits) // 2
    high, low = bits[half_bits:][::-1], bits[:half_bits][::-1]
    bits, swapped = [], []
    for i in range(len(high)):
        pair = high[i : i + 1] + low[i : i + 1]
        bits += pair
        swapped += pair[::-1]
    def near_chip(side):
        return call(
            chip_kernel,
            [stat_s, near_s],
            [q, near_kv, side],
            2 * 2 * rows * 2 * rows * width * 2,
            "near_chip",
            unread=(2,),
        )

    steps = len(bits)
    tied = {1: [q]}
    if steps < 3:
        stat, near = near_chip(side)
    for step in range(steps):
        def partner(n, step=step):
            return n ^ (1 << (swapped[step] if n % 2 else bits[step]))

        received = permute(msg, partner)
        if step < steps - 1:
            sums, side, msg = call(
                combine_kernel,
                [sums_s, side_s, msg_s],
                [sums, side, received] + tied.get(step, []),
                1000000,
                "slots_combine",
                unread=(3,),
            )
        if step == steps - 3:
            halo_own, side = lax.optimization_barrier((halo_own, side))
            stat, near = near_chip(side)
            tied[steps - 2] = [stat]
    halo_par = permute(halo_own, lambda n: n ^ 1)
    stat, near = call(
        functools.partial(halo_kernel, count),
        [stat_s, near_s],
        [halo_own, halo_par, wk, wv, q, stat, near, side],
        2 * 2 * rows * model * width * 2,
        "near_halo",
        unread=(7,),
    )
    send, slot_kv = call(
        far_partner_kernel,
        [((width, rows), BF16), ((half, feats, slots), BF16)],
        [sums, side, received, q, stat, near],
        2 * rows * slots * width * 2,
        "far_partner",
    )
    (part,) = call(
        far_own_kernel,
        [((rows, w_out.shape[1]), F32)],
        [slot_kv, q, stat, near, w_out],
        2 * rows * slots * width * 2,
        "far_own",
    )
    their_half = permute(send, lambda n: n ^ 1)
    (mixed,) = call(
        mix_kernel,
        [((rows, w_out.shape[1]), BF16)],
        [part, their_half, w_out],
        2 * rows * width * w_out.shape[1],
        "mix",
        sems=4,
        held=VMEM((rows, w_out.shape[1]), BF16),
    )
    return mixed


def solution(mesh):
    in_specs = (P(AXES, None), P(), P(), P(), P(), P())
    return jax.shard_map(
        per_device, mesh=mesh, in_specs=in_specs, out_specs=P(AXES, None), check_vma=False
    )
```

```python
import functools

import jax
import jax.numpy as jnp
from jax import lax
from jax.experimental import pallas as pl
from jax.experimental.pallas import tpu as pltpu
from jax.sharding import PartitionSpec as P

AXES = ("ctxa", "ctxb")
SIDE = 16
WINDOW = 128
EPS = 1e-05
BF16 = jnp.bfloat16
F32 = jnp.float32
VMEM = pltpu.VMEM


def dot(a, b, ca=1, cb=0):
    return lax.dot_general(a, b, (((ca,), (cb,)), ((), ())), preferred_element_type=F32)


def split_side(side):
    high = side.astype(BF16)
    rest = side - high.astype(F32)
    mid = rest.astype(BF16)
    low = rest - mid.astype(F32)
    parts = [high.astype(F32), mid.astype(F32), low, jnp.zeros_like(side)]
    return jnp.concatenate(parts, axis=0).astype(BF16)


def joined_side(msg_ref, at, rows):
    parts = msg_ref[at:, :].astype(F32)
    return parts[:rows] + parts[rows : 2 * rows] + parts[2 * rows : 3 * rows]


def merge(side_ref, msg_ref, heads, feats):
    own, other = side_ref[...], joined_side(msg_ref, heads * feats, 2 * heads)
    top = jnp.maximum(own[:heads], other[:heads])
    a, b = jnp.exp(own[:heads] - top), jnp.exp(other[:heads] - top)
    return top, own[heads:] * a + other[heads:] * b, a, b


def merged_sums(sums_ref, msg_ref, h, a, b):
    feats = sums_ref.shape[1]
    other = msg_ref[h * feats : (h + 1) * feats, :].astype(F32)
    return sums_ref[h] * a[h : h + 1] + other * b[h : h + 1]


def load_kernel(wk_all, wv_all, wk_ref, wv_ref, sems):
    width = wk_ref.shape[1]
    core = lax.axis_index(AXES) % 2
    cols = pl.ds(pl.multiple_of(core * width, width), width)
    copies = [
        pltpu.make_async_copy(wk_all.at[:, cols], wk_ref, sems.at[0]),
        pltpu.make_async_copy(wv_all.at[:, cols], wv_ref, sems.at[1]),
    ]
    for copy in copies:
        copy.start()
    for copy in copies:
        copy.wait()


def slots_kernel(own_ref, par_ref, wk_ref, wv_ref, ws_ref, sums_ref, side_ref, msg_ref, kv_ref):
    heads, feats, _ = kv_ref.shape
    dim = feats // 2
    first = lax.axis_index(AXES) % 2 * heads
    tokens = jnp.concatenate([own_ref[...], par_ref[...]], axis=0)
    key = dot(tokens, wk_ref[...]).astype(BF16)
    value = dot(tokens, wv_ref[...]).astype(BF16)
    key_t, value_t = key.T, value.T
    cols = [slice(h * dim, (h + 1) * dim) for h in range(heads)]
    logits = [dot(key[:, c], ws_ref[first + h]) for h, c in enumerate(cols)]
    pairs = [jnp.concatenate([key_t[c], value_t[c]], axis=0) for c in cols]
    tops = [jnp.max(x, axis=0, keepdims=True) for x in logits]
    weights = [jnp.exp(x - top) for x, top in zip(logits, tops)]
    totals = [jnp.sum(x, axis=0, keepdims=True) for x in weights]
    side = jnp.concatenate(tops + totals, axis=0)
    side_ref[...] = side
    msg_ref[heads * feats :, :] = split_side(side)
    for h in range(heads):
        kv_ref[h] = pairs[h]
        high = weights[h].astype(BF16)
        low = (weights[h] - high.astype(F32)).astype(BF16)
        both = dot(pairs[h], jnp.concatenate([high, low], axis=1))
        sums = both[:, : high.shape[1]] + both[:, high.shape[1] :]
        sums_ref[h] = sums
        msg_ref[h * feats : (h + 1) * feats, :] = sums.astype(BF16)


def combine_kernel(sums_ref, side_ref, msg_ref, *rest):
    sums_out, side_out, msg_out = rest[-3:]
    heads, feats, _ = sums_ref.shape
    top, total, a, b = merge(side_ref, msg_ref, heads, feats)
    side = jnp.concatenate([top, total], axis=0)
    side_out[...] = side
    msg_out[heads * feats :, :] = split_side(side)
    for h in range(heads):
        sums = merged_sums(sums_ref, msg_ref, h, a, b)
        sums_out[h] = sums
        msg_out[h * feats : (h + 1) * feats, :] = sums.astype(BF16)


def layer_norm_rows(u):
    center = u - jnp.mean(u, axis=0, keepdims=True)
    spread = jnp.mean(center * center, axis=0, keepdims=True)
    return center * lax.rsqrt(spread + EPS)


def query_kernel(own_ref, par_ref, wq_all, kv_ref, q_ref, near_ref, wq_ref, sems):
    width = wq_ref.shape[1]
    core = lax.axis_index(AXES) % 2
    cols = pl.ds(pl.multiple_of(core * width, width), width)
    copy = pltpu.make_async_copy(wq_all.at[:, cols], wq_ref, sems.at[0])
    copy.start()
    heads, both, _ = kv_ref.shape
    dim = both // 2
    near = [layer_norm_rows(kv_ref[h, :dim, :].astype(F32)).astype(BF16) for h in range(heads)]
    values = [kv_ref[h, dim:, :] for h in range(heads)]
    tokens = jnp.concatenate([own_ref[...], par_ref[...]], axis=0)
    copy.wait()
    q_ref[...] = dot(tokens, wq_ref[...]).astype(BF16).T
    for h in range(heads):
        near_ref[h, :dim, :] = near[h]
        near_ref[h, dim:, :] = values[h]


def sides(rows):
    core = lax.axis_index(AXES) % 2
    u = lax.broadcasted_iota(jnp.int32, (rows, rows), 0)
    t = lax.broadcasted_iota(jnp.int32, (rows, rows), 1)
    ahead = (u - t) * (1 - 2 * core)
    return ahead >= 0, ahead <= 0


def chip_kernel(q_ref, kv_ref, _, stat_ref, out_ref):
    heads, both, span = kv_ref.shape
    rows = span // 2
    dim = both // 2
    scale = 1.0 / dim**0.5
    before, after = sides(rows)
    scores = [
        dot(kv_ref[h, :dim, :], q_ref[h * dim : (h + 1) * dim, :], 0, 0) * scale
        for h in range(heads)
    ]
    items = [(h, part) for part in range(2) for h in range(heads)]
    halves = [
        (
            scores[h][:rows, :rows] if part == 0 else jnp.where(before, scores[h][:rows, rows:], -1e30),
            scores[h][rows:, rows:] if part == 1 else jnp.where(after, scores[h][rows:, :rows], -1e30),
        )
        for h, part in items
    ]
    tops = [jnp.max(jnp.maximum(s0, s1), axis=0, keepdims=True) for s0, s1 in halves]
    exps = [(jnp.exp(s0 - top), jnp.exp(s1 - top)) for (s0, s1), top in zip(halves, tops)]
    totals = [jnp.sum(e0 + e1, axis=0, keepdims=True) for e0, e1 in exps]
    wide = [jnp.concatenate([e0.astype(BF16), e1.astype(BF16)], axis=0) for e0, e1 in exps]
    outs = [
        dot(kv_ref[h, dim:, :], jnp.concatenate([wide[h], wide[heads + h]], axis=1))
        for h in range(heads)
    ]
    for part in range(2):
        of = slice(part * heads, (part + 1) * heads)
        stat_ref[part] = jnp.concatenate(tops[of] + totals[of], axis=0)
        out_ref[part] = jnp.concatenate([x[:, part * rows : (part + 1) * rows] for x in outs], axis=0)


def halo_kernel(n_dev, hown_ref, hpar_ref, wk_ref, wv_ref, q_ref, chip_stat, chip_out, _, stat_ref, out_ref):
    rows = hown_ref.shape[0]
    width = wk_ref.shape[1]
    heads = stat_ref.shape[1] // 2
    dim = width // heads
    scale = 1.0 / dim**0.5
    tokens = jnp.concatenate([hown_ref[...], hpar_ref[...]], axis=0)
    key_t = dot(tokens, wk_ref[...]).astype(BF16).T
    value_t = dot(tokens, wv_ref[...]).astype(BF16).T
    me = lax.axis_index(AXES)
    first, last = me >= 2, me < n_dev - 2
    even = me % 2 == 0
    before, after = sides(rows)
    valid = [
        before & ((even & first) | (~even & last)),
        after & ((even & last) | (~even & first)),
    ]
    feats = [slice(h * dim, (h + 1) * dim) for h in range(heads)]
    cols = [slice(part * rows, (part + 1) * rows) for part in range(2)]
    near_keys = [layer_norm_rows(key_t[f].astype(F32)).astype(BF16) for f in feats]
    items = [(h, part) for part in range(2) for h in range(heads)]
    scores = [
        jnp.where(
            valid[part], dot(near_keys[h][:, cols[part]], q_ref[feats[h], cols[part]], 0, 0) * scale, -1e30
        )
        for h, part in items
    ]
    old_tops = [chip_stat[part, h : h + 1, :] for h, part in items]
    tops = [jnp.maximum(jnp.max(s, axis=0, keepdims=True), t) for s, t in zip(scores, old_tops)]
    old_scales = [jnp.exp(t - top) for t, top in zip(old_tops, tops)]
    exps = [jnp.exp(s - top) for s, top in zip(scores, tops)]
    totals = [
        chip_stat[part, heads + h : heads + h + 1, :] * a + jnp.sum(e, axis=0, keepdims=True)
        for (h, part), a, e in zip(items, old_scales, exps)
    ]
    outs = [
        chip_out[part, feats[h], :] * a + dot(value_t[feats[h], cols[part]], e.astype(BF16))
        for (h, part), a, e in zip(items, old_scales, exps)
    ]
    for part in range(2):
        of = slice(part * heads, (part + 1) * heads)
        stat_ref[part] = jnp.concatenate(tops[of] + totals[of], axis=0)
        out_ref[part] = jnp.concatenate(outs[of], axis=0)


def far_rows(part, slots, q_ref, stat_ref, near_ref):
    heads = len(slots)
    dim = slots[0][0].shape[0]
    rows = near_ref.shape[2]
    feats = [slice(h * dim, (h + 1) * dim) for h in range(heads)]
    cols = slice(part * rows, (part + 1) * rows)
    scale = 1.0 / dim**0.5
    far = [dot(keys, q_ref[f, cols], 0, 0) * scale for (keys, _), f in zip(slots, feats)]
    near_tops = [stat_ref[part, h : h + 1, :] for h in range(heads)]
    tops = [jnp.maximum(jnp.max(x, axis=0, keepdims=True), t) for x, t in zip(far, near_tops)]
    near_scales = [jnp.exp(t - top) for t, top in zip(near_tops, tops)]
    exps = [jnp.exp(x - top) for x, top in zip(far, tops)]
    denoms = [
        jnp.sum(e, axis=0, keepdims=True) + stat_ref[part, heads + h : heads + h + 1, :] * near_scales[h]
        for h, e in enumerate(exps)
    ]
    outs = [
        near_ref[part, f, :] * a + dot(values, e.astype(BF16))
        for f, a, (_, values), e in zip(feats, near_scales, slots, exps)
    ]
    return jnp.concatenate([(x / d).astype(BF16) for x, d in zip(outs, denoms)], axis=0)


def far_partner_kernel(sums_ref, side_ref, msg_ref, q_ref, stat_ref, near_ref, send_ref, slots_ref):
    heads, feats, _ = sums_ref.shape
    dim = feats // 2
    _, total, a, b = merge(side_ref, msg_ref, heads, feats)
    sums = [merged_sums(sums_ref, msg_ref, h, a, b) for h in range(heads)]
    slots = [
        (layer_norm_rows(x[:dim]).astype(BF16), (x[dim:] / total[h : h + 1]).astype(BF16))
        for h, x in enumerate(sums)
    ]
    send_ref[...] = far_rows(1, slots, q_ref, stat_ref, near_ref)
    for h, (keys, values) in enumerate(slots):
        slots_ref[h, :dim, :] = keys
        slots_ref[h, dim:, :] = values


def far_own_kernel(slots_ref, q_ref, stat_ref, near_ref, w_ref, out_ref):
    heads, feats, _ = slots_ref.shape
    dim = feats // 2
    width = heads * dim
    core = lax.axis_index(AXES) % 2
    slots = [(slots_ref[h, :dim, :], slots_ref[h, dim:, :]) for h in range(heads)]
    rows = far_rows(0, slots, q_ref, stat_ref, near_ref)
    mine = pl.ds(pl.multiple_of(core * width, width), width)
    out_ref[...] = dot(rows, w_ref[mine, :], 0, 0)


def mix_kernel(part_ref, other_ref, w_ref, out_ref, held_ref, sems):
    width = other_ref.shape[0]
    pieces = sems.shape[0]
    cols = out_ref.shape[1] // pieces
    core = lax.axis_index(AXES) % 2
    theirs = pl.ds(pl.multiple_of((1 - core) * width, width), width)
    other = other_ref[...].T
    copies = []
    for i in range(pieces):
        at = slice(i * cols, (i + 1) * cols)
        held_ref[:, at] = (part_ref[:, at] + dot(other, w_ref[theirs, at])).astype(BF16)
        copies.append(pltpu.make_async_copy(held_ref.at[:, at], out_ref.at[:, at], sems.at[i]))
        copies[i].start()
    for copy in copies:
        copy.wait()


def call(kernel, outs, ins, flops, name, unread=(), hbm=(), sems=0, grant=24, held=None, scratch=None):
    spec = pl.BlockSpec(memory_space=VMEM)
    anywhere = pl.BlockSpec(memory_space=pl.ANY)
    stays = pl.BlockSpec(memory_space=pltpu.HBM)
    out_shape = [jax.ShapeDtypeStruct(s, d) for s, d in outs]
    size = sum(x.size * x.dtype.itemsize for x in ins) + sum(
        s.size * s.dtype.itemsize for s in out_shape
    )
    return pl.pallas_call(
        kernel,
        out_shape=out_shape,
        in_specs=[anywhere if i in unread else stays if i in hbm else spec for i in range(len(ins))],
        out_specs=[stays if held else spec] * len(outs),
        scratch_shapes=[x for x in (held, scratch) if x] + ([pltpu.SemaphoreType.DMA((sems,))] if sems else []),
        compiler_params=pltpu.CompilerParams(vmem_limit_bytes=grant * 2**20),
        cost_estimate=pl.CostEstimate(flops=flops, bytes_accessed=size, transcendentals=0),
        name=name,
    )(*ins)


def per_device(tokens, w_query, w_key, w_value, w_slot, w_out):
    rows, model = tokens.shape
    count = lax.axis_size(AXES)
    heads, dim, slots = w_slot.shape
    half = heads // 2
    width = half * dim
    feats = 2 * dim

    def permute(x, target):
        pairs = [(n, target(n)) for n in range(count) if 0 <= target(n) < count]
        return lax.ppermute(x, AXES, pairs)

    weight_s = ((model, width), BF16)
    sums_s, side_s = ((half, feats, slots), F32), ((2 * half, slots), F32)
    msg_s = ((half * feats + 8 * half, slots), BF16)
    chunk_s = ((half, feats, rows), BF16)
    stat_s, near_s = ((2, 2 * half, rows), F32), ((2, width, rows), F32)

    other = permute(tokens, lambda n: n ^ 1)
    wk, wv = call(
        load_kernel,
        [weight_s, weight_s],
        [w_key, w_value],
        0,
        "load",
        hbm=(0, 1),
        sems=2,
        grant=52,
    )
    sums, side, msg, kv = call(
        slots_kernel,
        [sums_s, side_s, msg_s, ((half, feats, 2 * rows), BF16)],
        [tokens, other, wk, wv, w_slot],
        2 * 2 * rows * model * width * 2,
        "slots_local",
    )
    q, near_kv = call(
        query_kernel,
        [((width, 2 * rows), BF16), ((half, feats, 2 * rows), BF16)],
        [tokens, other, w_query, kv],
        2 * 2 * rows * model * width,
        "query_norm",
        hbm=(2,),
        sems=1,
        scratch=VMEM((model, width), BF16),
    )
    halo_own = permute(tokens, lambda n: n - 1 + 2 * (n % 2))
    bits = list(range(1, (count - 1).bit_length()))
    low, high = bits[: len(bits) // 2], bits[len(bits) // 2 :][::-1]
    bits, swapped = high + low, low + high

    def near_chip(side):
        return call(
            chip_kernel,
            [stat_s, near_s],
            [q, near_kv, side],
            2 * 2 * rows * 2 * rows * width * 2,
            "near_chip",
            unread=(2,),
        )

    steps = len(bits)
    tied = {1: [q]}
    if steps < 3:
        stat, near = near_chip(side)
    for step in range(steps):
        def partner(n, step=step):
            return n ^ (1 << (swapped[step] if n % 2 else bits[step]))

        received = permute(msg, partner)
        if step < steps - 1:
            sums, side, msg = call(
                combine_kernel,
                [sums_s, side_s, msg_s],
                [sums, side, received] + tied.get(step, []),
                1000000,
                "slots_combine",
                unread=(3,),
            )
        if step == steps - 3:
            halo_own, side = lax.optimization_barrier((halo_own, side))
            stat, near = near_chip(side)
            tied[steps - 2] = [stat]
    halo_par = permute(halo_own, lambda n: n ^ 1)
    stat, near = call(
        functools.partial(halo_kernel, count),
        [stat_s, near_s],
        [halo_own, halo_par, wk, wv, q, stat, near, side],
        2 * 2 * rows * model * width * 2,
        "near_halo",
        unread=(7,),
    )
    send, slot_kv = call(
        far_partner_kernel,
        [((width, rows), BF16), ((half, feats, slots), BF16)],
        [sums, side, received, q, stat, near],
        2 * rows * slots * width * 2,
        "far_partner",
    )
    (part,) = call(
        far_own_kernel,
        [((rows, w_out.shape[1]), F32)],
        [slot_kv, q, stat, near, w_out],
        2 * rows * slots * width * 2,
        "far_own",
    )
    their_half = permute(send, lambda n: n ^ 1)
    (mixed,) = call(
        mix_kernel,
        [((rows, w_out.shape[1]), BF16)],
        [part, their_half, w_out],
        2 * rows * width * w_out.shape[1],
        "mix",
        sems=4,
        held=VMEM((rows, w_out.shape[1]), BF16),
    )
    return mixed


def solution(mesh):
    in_specs = (P(AXES, None), P(), P(), P(), P(), P())
    return jax.shard_map(
        per_device, mesh=mesh, in_specs=in_specs, out_specs=P(AXES, None), check_vma=False
    )
```

```python
import functools

import jax
import jax.numpy as jnp
from jax import lax
from jax.experimental import pallas as pl
from jax.experimental.pallas import tpu as pltpu
from jax.sharding import PartitionSpec as P

AXES = ("ctxa", "ctxb")
SIDE = 16
WINDOW = 128
EPS = 1e-05
BF16 = jnp.bfloat16
F32 = jnp.float32
VMEM = pltpu.VMEM


def dot(a, b, ca=1, cb=0):
    return lax.dot_general(a, b, (((ca,), (cb,)), ((), ())), preferred_element_type=F32)


def split_side(side):
    high = side.astype(BF16)
    rest = side - high.astype(F32)
    mid = rest.astype(BF16)
    low = rest - mid.astype(F32)
    parts = [high.astype(F32), mid.astype(F32), low, jnp.zeros_like(side)]
    return jnp.concatenate(parts, axis=0).astype(BF16)


def joined_side(msg_ref, at, rows):
    parts = msg_ref[at:, :].astype(F32)
    return parts[:rows] + parts[rows : 2 * rows] + parts[2 * rows : 3 * rows]


def merge(side_ref, msg_ref, heads, feats):
    own, other = side_ref[...], joined_side(msg_ref, heads * feats, 2 * heads)
    top = jnp.maximum(own[:heads], other[:heads])
    a, b = jnp.exp(own[:heads] - top), jnp.exp(other[:heads] - top)
    return top, own[heads:] * a + other[heads:] * b, a, b


def merged_sums(sums_ref, msg_ref, h, a, b):
    feats = sums_ref.shape[1]
    other = msg_ref[h * feats : (h + 1) * feats, :].astype(F32)
    return sums_ref[h] * a[h : h + 1] + other * b[h : h + 1]


def load_kernel(wk_all, wv_all, wk_ref, wv_ref, sems):
    width = wk_ref.shape[1]
    core = lax.axis_index(AXES) % 2
    cols = pl.ds(pl.multiple_of(core * width, width), width)
    copies = [
        pltpu.make_async_copy(wk_all.at[:, cols], wk_ref, sems.at[0]),
        pltpu.make_async_copy(wv_all.at[:, cols], wv_ref, sems.at[1]),
    ]
    for copy in copies:
        copy.start()
    for copy in copies:
        copy.wait()


def slots_kernel(own_ref, par_ref, wk_ref, wv_ref, ws_ref, sums_ref, side_ref, msg_ref, kv_ref, edge_ref):
    heads, feats, _ = kv_ref.shape
    dim = feats // 2
    me = lax.axis_index(AXES)
    first = me % 2 * heads
    edge_ref[...] = jnp.where(me // 2 % 2 == 1, own_ref[...], par_ref[...])
    tokens = jnp.concatenate([own_ref[...], par_ref[...]], axis=0)
    key = dot(tokens, wk_ref[...]).astype(BF16)
    value = dot(tokens, wv_ref[...]).astype(BF16)
    key_t, value_t = key.T, value.T
    cols = [slice(h * dim, (h + 1) * dim) for h in range(heads)]
    logits = [dot(key[:, c], ws_ref[first + h]) for h, c in enumerate(cols)]
    pairs = [jnp.concatenate([key_t[c], value_t[c]], axis=0) for c in cols]
    tops = [jnp.max(x, axis=0, keepdims=True) for x in logits]
    weights = [jnp.exp(x - top) for x, top in zip(logits, tops)]
    totals = [jnp.sum(x, axis=0, keepdims=True) for x in weights]
    side = jnp.concatenate(tops + totals, axis=0)
    side_ref[...] = side
    msg_ref[heads * feats :, :] = split_side(side)
    for h in range(heads):
        kv_ref[h] = pairs[h]
        high = weights[h].astype(BF16)
        low = (weights[h] - high.astype(F32)).astype(BF16)
        both = dot(pairs[h], jnp.concatenate([high, low], axis=1))
        sums = both[:, : high.shape[1]] + both[:, high.shape[1] :]
        sums_ref[h] = sums
        msg_ref[h * feats : (h + 1) * feats, :] = sums.astype(BF16)


def combine_kernel(sums_ref, side_ref, msg_ref, *rest):
    sums_out, side_out, msg_out = rest[-3:]
    heads, feats, _ = sums_ref.shape
    top, total, a, b = merge(side_ref, msg_ref, heads, feats)
    side = jnp.concatenate([top, total], axis=0)
    side_out[...] = side
    msg_out[heads * feats :, :] = split_side(side)
    for h in range(heads):
        sums = merged_sums(sums_ref, msg_ref, h, a, b)
        sums_out[h] = sums
        msg_out[h * feats : (h + 1) * feats, :] = sums.astype(BF16)


def layer_norm_rows(u):
    center = u - jnp.mean(u, axis=0, keepdims=True)
    spread = jnp.mean(center * center, axis=0, keepdims=True)
    return center * lax.rsqrt(spread + EPS)


def query_kernel(own_ref, par_ref, wq_all, kv_ref, q_ref, near_ref, wq_ref, sems):
    width = wq_ref.shape[1]
    core = lax.axis_index(AXES) % 2
    cols = pl.ds(pl.multiple_of(core * width, width), width)
    copy = pltpu.make_async_copy(wq_all.at[:, cols], wq_ref, sems.at[0])
    copy.start()
    heads, both, _ = kv_ref.shape
    dim = both // 2
    near = [layer_norm_rows(kv_ref[h, :dim, :].astype(F32)).astype(BF16) for h in range(heads)]
    values = [kv_ref[h, dim:, :] for h in range(heads)]
    tokens = jnp.concatenate([own_ref[...], par_ref[...]], axis=0)
    copy.wait()
    q_ref[...] = dot(tokens, wq_ref[...]).astype(BF16).T
    for h in range(heads):
        near_ref[h, :dim, :] = near[h]
        near_ref[h, dim:, :] = values[h]


def sides(rows):
    core = lax.axis_index(AXES) % 2
    u = lax.broadcasted_iota(jnp.int32, (rows, rows), 0)
    t = lax.broadcasted_iota(jnp.int32, (rows, rows), 1)
    ahead = (u - t) * (1 - 2 * core)
    return ahead >= 0, ahead <= 0


def chip_kernel(q_ref, kv_ref, _, stat_ref, out_ref):
    heads, both, span = kv_ref.shape
    rows = span // 2
    dim = both // 2
    scale = 1.0 / dim**0.5
    before, after = sides(rows)
    scores = [
        dot(kv_ref[h, :dim, :], q_ref[h * dim : (h + 1) * dim, :], 0, 0) * scale
        for h in range(heads)
    ]
    items = [(h, part) for part in range(2) for h in range(heads)]
    halves = [
        (
            scores[h][:rows, :rows] if part == 0 else jnp.where(before, scores[h][:rows, rows:], -1e30),
            scores[h][rows:, rows:] if part == 1 else jnp.where(after, scores[h][rows:, :rows], -1e30),
        )
        for h, part in items
    ]
    tops = [jnp.max(jnp.maximum(s0, s1), axis=0, keepdims=True) for s0, s1 in halves]
    exps = [(jnp.exp(s0 - top), jnp.exp(s1 - top)) for (s0, s1), top in zip(halves, tops)]
    totals = [jnp.sum(e0 + e1, axis=0, keepdims=True) for e0, e1 in exps]
    wide = [jnp.concatenate([e0.astype(BF16), e1.astype(BF16)], axis=0) for e0, e1 in exps]
    outs = [
        dot(kv_ref[h, dim:, :], jnp.concatenate([wide[h], wide[heads + h]], axis=1))
        for h in range(heads)
    ]
    for part in range(2):
        of = slice(part * heads, (part + 1) * heads)
        stat_ref[part] = jnp.concatenate(tops[of] + totals[of], axis=0)
        out_ref[part] = jnp.concatenate([x[:, part * rows : (part + 1) * rows] for x in outs], axis=0)


def halo_kernel(n_dev, halo_ref, other_ref, wk_ref, wv_ref, q_ref, chip_stat, chip_out, _, stat_ref, out_ref):
    rows = halo_ref.shape[0]
    width = wk_ref.shape[1]
    heads = stat_ref.shape[1] // 2
    dim = width // heads
    scale = 1.0 / dim**0.5
    me = lax.axis_index(AXES)
    swap = me // 2 % 2 == 0
    halo, other = halo_ref[...], other_ref[...]
    tokens = jnp.concatenate([jnp.where(swap, other, halo), jnp.where(swap, halo, other)], axis=0)
    key_t = dot(tokens, wk_ref[...]).astype(BF16).T
    value_t = dot(tokens, wv_ref[...]).astype(BF16).T
    first, last = me >= 2, me < n_dev - 2
    even = me % 2 == 0
    before, after = sides(rows)
    valid = [
        before & ((even & first) | (~even & last)),
        after & ((even & last) | (~even & first)),
    ]
    feats = [slice(h * dim, (h + 1) * dim) for h in range(heads)]
    cols = [slice(part * rows, (part + 1) * rows) for part in range(2)]
    near_keys = [layer_norm_rows(key_t[f].astype(F32)).astype(BF16) for f in feats]
    items = [(h, part) for part in range(2) for h in range(heads)]
    scores = [
        jnp.where(
            valid[part], dot(near_keys[h][:, cols[part]], q_ref[feats[h], cols[part]], 0, 0) * scale, -1e30
        )
        for h, part in items
    ]
    old_tops = [chip_stat[part, h : h + 1, :] for h, part in items]
    tops = [jnp.maximum(jnp.max(s, axis=0, keepdims=True), t) for s, t in zip(scores, old_tops)]
    old_scales = [jnp.exp(t - top) for t, top in zip(old_tops, tops)]
    exps = [jnp.exp(s - top) for s, top in zip(scores, tops)]
    totals = [
        chip_stat[part, heads + h : heads + h + 1, :] * a + jnp.sum(e, axis=0, keepdims=True)
        for (h, part), a, e in zip(items, old_scales, exps)
    ]
    outs = [
        chip_out[part, feats[h], :] * a + dot(value_t[feats[h], cols[part]], e.astype(BF16))
        for (h, part), a, e in zip(items, old_scales, exps)
    ]
    for part in range(2):
        of = slice(part * heads, (part + 1) * heads)
        stat_ref[part] = jnp.concatenate(tops[of] + totals[of], axis=0)
        out_ref[part] = jnp.concatenate(outs[of], axis=0)


def far_rows(part, slots, q_ref, stat_ref, near_ref):
    heads = len(slots)
    dim = slots[0][0].shape[0]
    rows = near_ref.shape[2]
    feats = [slice(h * dim, (h + 1) * dim) for h in range(heads)]
    cols = slice(part * rows, (part + 1) * rows)
    scale = 1.0 / dim**0.5
    far = [dot(keys, q_ref[f, cols], 0, 0) * scale for (keys, _), f in zip(slots, feats)]
    near_tops = [stat_ref[part, h : h + 1, :] for h in range(heads)]
    tops = [jnp.maximum(jnp.max(x, axis=0, keepdims=True), t) for x, t in zip(far, near_tops)]
    near_scales = [jnp.exp(t - top) for t, top in zip(near_tops, tops)]
    exps = [jnp.exp(x - top) for x, top in zip(far, tops)]
    denoms = [
        jnp.sum(e, axis=0, keepdims=True) + stat_ref[part, heads + h : heads + h + 1, :] * near_scales[h]
        for h, e in enumerate(exps)
    ]
    outs = [
        near_ref[part, f, :] * a + dot(values, e.astype(BF16))
        for f, a, (_, values), e in zip(feats, near_scales, slots, exps)
    ]
    return jnp.concatenate([(x / d).astype(BF16) for x, d in zip(outs, denoms)], axis=0)


def far_partner_kernel(sums_ref, side_ref, msg_ref, q_ref, stat_ref, near_ref, send_ref, slots_ref):
    heads, feats, _ = sums_ref.shape
    dim = feats // 2
    _, total, a, b = merge(side_ref, msg_ref, heads, feats)
    sums = [merged_sums(sums_ref, msg_ref, h, a, b) for h in range(heads)]
    slots = [
        (layer_norm_rows(x[:dim]).astype(BF16), (x[dim:] / total[h : h + 1]).astype(BF16))
        for h, x in enumerate(sums)
    ]
    send_ref[...] = far_rows(1, slots, q_ref, stat_ref, near_ref)
    for h, (keys, values) in enumerate(slots):
        slots_ref[h, :dim, :] = keys
        slots_ref[h, dim:, :] = values


def far_own_kernel(slots_ref, q_ref, stat_ref, near_ref, w_ref, out_ref):
    heads, feats, _ = slots_ref.shape
    dim = feats // 2
    width = heads * dim
    core = lax.axis_index(AXES) % 2
    slots = [(slots_ref[h, :dim, :], slots_ref[h, dim:, :]) for h in range(heads)]
    rows = far_rows(0, slots, q_ref, stat_ref, near_ref)
    mine = pl.ds(pl.multiple_of(core * width, width), width)
    out_ref[...] = dot(rows, w_ref[mine, :], 0, 0)


def mix_kernel(part_ref, other_ref, w_ref, out_ref, held_ref, sems):
    width = other_ref.shape[0]
    pieces = sems.shape[0]
    cols = out_ref.shape[1] // pieces
    core = lax.axis_index(AXES) % 2
    theirs = pl.ds(pl.multiple_of((1 - core) * width, width), width)
    other = other_ref[...].T
    copies = []
    for i in range(pieces):
        at = slice(i * cols, (i + 1) * cols)
        held_ref[:, at] = (part_ref[:, at] + dot(other, w_ref[theirs, at])).astype(BF16)
        copies.append(pltpu.make_async_copy(held_ref.at[:, at], out_ref.at[:, at], sems.at[i]))
        copies[i].start()
    for copy in copies:
        copy.wait()


def call(kernel, outs, ins, flops, name, unread=(), hbm=(), sems=0, grant=24, held=None, scratch=None):
    spec = pl.BlockSpec(memory_space=VMEM)
    anywhere = pl.BlockSpec(memory_space=pl.ANY)
    stays = pl.BlockSpec(memory_space=pltpu.HBM)
    out_shape = [jax.ShapeDtypeStruct(s, d) for s, d in outs]
    size = sum(x.size * x.dtype.itemsize for x in ins) + sum(
        s.size * s.dtype.itemsize for s in out_shape
    )
    return pl.pallas_call(
        kernel,
        out_shape=out_shape,
        in_specs=[anywhere if i in unread else stays if i in hbm else spec for i in range(len(ins))],
        out_specs=[stays if held else spec] * len(outs),
        scratch_shapes=[x for x in (held, scratch) if x] + ([pltpu.SemaphoreType.DMA((sems,))] if sems else []),
        compiler_params=pltpu.CompilerParams(vmem_limit_bytes=grant * 2**20),
        cost_estimate=pl.CostEstimate(flops=flops, bytes_accessed=size, transcendentals=0),
        name=name,
    )(*ins)


def per_device(tokens, w_query, w_key, w_value, w_slot, w_out):
    rows, model = tokens.shape
    count = lax.axis_size(AXES)
    heads, dim, slots = w_slot.shape
    half = heads // 2
    width = half * dim
    feats = 2 * dim

    def permute(x, target):
        pairs = [(n, target(n)) for n in range(count) if 0 <= target(n) < count]
        return lax.ppermute(x, AXES, pairs)

    weight_s = ((model, width), BF16)
    sums_s, side_s = ((half, feats, slots), F32), ((2 * half, slots), F32)
    msg_s = ((half * feats + 8 * half, slots), BF16)
    chunk_s = ((half, feats, rows), BF16)
    stat_s, near_s = ((2, 2 * half, rows), F32), ((2, width, rows), F32)

    other = permute(tokens, lambda n: n ^ 1)
    wk, wv = call(
        load_kernel,
        [weight_s, weight_s],
        [w_key, w_value],
        0,
        "load",
        hbm=(0, 1),
        sems=2,
        grant=52,
    )
    sums, side, msg, kv, edge = call(
        slots_kernel,
        [sums_s, side_s, msg_s, ((half, feats, 2 * rows), BF16), ((rows, model), BF16)],
        [tokens, other, wk, wv, w_slot],
        2 * 2 * rows * model * width * 2,
        "slots_local",
    )
    q, near_kv = call(
        query_kernel,
        [((width, 2 * rows), BF16), ((half, feats, 2 * rows), BF16)],
        [tokens, other, w_query, kv],
        2 * 2 * rows * model * width,
        "query_norm",
        hbm=(2,),
        sems=1,
        scratch=VMEM((model, width), BF16),
    )
    halo = permute(edge, lambda n: n + 2 if (n // 2 + n) % 2 == 0 else n - 2)
    bits = list(range(1, (count - 1).bit_length()))
    low, high = bits[: len(bits) // 2], bits[len(bits) // 2 :][::-1]
    bits, swapped = high + low, low + high

    def near_chip(side):
        return call(
            chip_kernel,
            [stat_s, near_s],
            [q, near_kv, side],
            2 * 2 * rows * 2 * rows * width * 2,
            "near_chip",
            unread=(2,),
        )

    steps = len(bits)
    tied = {1: [q]}
    if steps < 3:
        stat, near = near_chip(side)
    for step in range(steps):
        def partner(n, step=step):
            return n ^ (1 << (swapped[step] if n % 2 else bits[step]))

        received = permute(msg, partner)
        if step < steps - 1:
            sums, side, msg = call(
                combine_kernel,
                [sums_s, side_s, msg_s],
                [sums, side, received] + tied.get(step, []),
                1000000,
                "slots_combine",
                unread=(3,),
            )
        if step == steps - 3:
            halo, side = lax.optimization_barrier((halo, side))
            stat, near = near_chip(side)
            tied[steps - 2] = [stat]
    other_halo = permute(halo, lambda n: n ^ 1)
    stat, near = call(
        functools.partial(halo_kernel, count),
        [stat_s, near_s],
        [halo, other_halo, wk, wv, q, stat, near, side],
        2 * 2 * rows * model * width * 2,
        "near_halo",
        unread=(7,),
    )
    send, slot_kv = call(
        far_partner_kernel,
        [((width, rows), BF16), ((half, feats, slots), BF16)],
        [sums, side, received, q, stat, near],
        2 * rows * slots * width * 2,
        "far_partner",
    )
    (part,) = call(
        far_own_kernel,
        [((rows, w_out.shape[1]), F32)],
        [slot_kv, q, stat, near, w_out],
        2 * rows * slots * width * 2,
        "far_own",
    )
    their_half = permute(send, lambda n: n ^ 1)
    (mixed,) = call(
        mix_kernel,
        [((rows, w_out.shape[1]), BF16)],
        [part, their_half, w_out],
        2 * rows * width * w_out.shape[1],
        "mix",
        sems=4,
        held=VMEM((rows, w_out.shape[1]), BF16),
    )
    return mixed


def solution(mesh):
    in_specs = (P(AXES, None), P(), P(), P(), P(), P())
    return jax.shard_map(
        per_device, mesh=mesh, in_specs=in_specs, out_specs=P(AXES, None), check_vma=False
    )
```
